32 devices in a mesh: nodes: 16 (over z, y, x), mp: 2 (over core).
Axes of the slice: x: 2, y: 2, z: 4, core: 2. Of those that a mesh axis runs over, the one named last changes fastest.
Arguments:
- memory: bfloat16 [32768, 512], P('nodes'), may hold values from -6 to 6
- ev_time: int32 [2048], P('nodes'), may hold values from 0 to 1023
- nbr_time: int32 [2048, 2, 16], P('nodes'), may hold values from 0 to 1023
- edge_feat: bfloat16 [2048, 128], P('nodes', 'mp'), may hold values from -6 to 6
- self_slot: int32 [2048, 2], P('nodes'), may hold values from 0 to 511
- nbr_slot: int32 [2048, 2, 16], P('nodes'), may hold values from 0 to 511
- serve_self: int32 [16, 16, 32], P('nodes'), may hold values from 0 to 2047
- serve_rows: int32 [16, 16, 32], P('nodes'), may hold values from 0 to 2047
- freq: float32 [128], replicated, may hold values from 0.001 to 0.5
- phase: float32 [128], replicated, may hold values from -3.140625 to 3.140625
- w_query: bfloat16 [640, 512], P(None, 'mp'), may hold values from -0.25 to 0.25
- w_key: bfloat16 [640, 512], P(None, 'mp'), may hold values from -0.25 to 0.25
- w_value: bfloat16 [640, 512], P(None, 'mp'), may hold values from -0.25 to 0.25
- w_out: bfloat16 [512, 512], P('mp'), may hold values from -0.25 to 0.25
- w_self: bfloat16 [512, 512], P('mp'), may hold values from -0.25 to 0.25
- w_msg_self: bfloat16 [512, 512], P('mp'), may hold values from -0.25 to 0.25
- w_msg_other: bfloat16 [512, 512], P('mp'), may hold values from -0.25 to 0.25
- w_msg_time: bfloat16 [128, 512], P('mp'), may hold values from -0.5 to 0.5
- w_msg_edge: bfloat16 [128, 512], P('mp'), may hold values from -0.5 to 0.5
- w_in: bfloat16 [512, 3, 512], P(None, None, 'mp'), may hold values from -0.25 to 0.25
- w_hid: bfloat16 [512, 3, 512], P(None, None, 'mp'), may hold values from -0.25 to 0.25
Outputs:
- embedding: bfloat16 [2048, 2, 512], P('nodes')
- memory_out: bfloat16 [32768, 512], P('nodes', 'mp')
The draws below stay inside these ranges and needn't reach their ends.
Inputs may be any that keep to these rules, and one draw needn't show every extreme that they name: `self_slot`: slot index o * 32 + s refers to endpoint slot s of owner o. `nbr_slot`: slot index o * 32 + s refers to neighbour slot s of owner o.
All inputs are finite; a program needn't handle non-finite values.
Results may differ from the reference program's by a relative error of at most 0.0075.
Values may be sent and summed in bfloat16 or wider, within the bound.
No kernel may reach another device: no remote copies, remote signals or barrier semaphores. Data moves between devices by JAX's collectives and lax.ppermute only.
A program may use at most 128 MiB of HBM per device.

```python
import math
import jax
import jax.numpy as jnp
from jax import lax

W = 512
HEADS = 8
HEAD = 64
K = 16
TD = 128
EF = 128
MSG = 512
BINS = 1024
EV_DEV = 128
ROWS_DEV = 2048
CAP = 32
CAP_SELF = 32
PEERS = 16
EVENTS = 2048
NODES = 32768


def place_ends(result, own_key, smallest, largest):
    index_at = [jax.random.randint(jax.random.fold_in(own_key, axis), (), 0, length) for axis, length in enumerate(result.shape)]
    longest = result.shape.index(max(result.shape))
    neighbour = index_at[:longest] + [(index_at[longest] + 1) % result.shape[longest]] + index_at[longest + 1:]
    return result.at[tuple(index_at)].set(smallest).at[tuple(neighbour)].set(largest)


def steps_of(stream_key, extent, split, smallest, high):
    def one(dim, blocks):
        heights = jax.random.uniform(jax.random.fold_in(jax.random.fold_in(stream_key, 6), dim), (blocks,), jnp.float32, smallest / len(split), high / len(split))
        return jnp.repeat(jnp.exp(heights), extent[dim] // blocks).reshape((-1,) + (1,) * (len(extent) - dim - 1))

    gain = one(*split[0])
    for cut in split[1:]:
        gain = gain * one(*cut)
    return gain


def gaussian(key, shape, scale, reach, shards=(), kind=jnp.bfloat16):
    result = scale * jax.random.normal(key, shape, jnp.float32)
    if shards:
        result = result * steps_of(key, shape, shards, -0.22, 0.18)
    return jnp.clip(result, -reach, reach).astype(kind)


def setup_inputs(seed: int = 0) -> dict:
    splits = jax.random.split(jax.random.key(seed), 22)
    return {
        "memory": gaussian(splits[0], (NODES, W), 1.0, 6.0, ((0, 16),)),
        "ev_time": place_ends(jax.random.randint(splits[1], (EVENTS,), 0, BINS), jax.random.fold_in(splits[1], 1), 0, BINS - 1).astype(jnp.int32),
        "nbr_time": place_ends(jax.random.randint(splits[2], (EVENTS, 2, K), 0, BINS), jax.random.fold_in(splits[2], 1), 0, BINS - 1).astype(jnp.int32),
        "edge_feat": gaussian(splits[3], (EVENTS, EF), 1.0, 6.0, ((0, 16), (1, 2))),
        "self_slot": place_ends(jax.random.randint(splits[4], (EVENTS, 2), 0, PEERS * CAP_SELF), jax.random.fold_in(splits[4], 1), 0, (PEERS * CAP_SELF) - 1).astype(jnp.int32),
        "nbr_slot": place_ends(jax.random.randint(splits[5], (EVENTS, 2, K), 0, PEERS * CAP), jax.random.fold_in(splits[5], 1), 0, (PEERS * CAP) - 1).astype(jnp.int32),
        "serve_self": place_ends(jax.random.randint(splits[6], (PEERS, PEERS, CAP_SELF), 0, ROWS_DEV), jax.random.fold_in(splits[6], 1), 0, ROWS_DEV - 1).astype(jnp.int32),
        "serve_rows": place_ends(jax.random.randint(splits[7], (PEERS, PEERS, CAP), 0, ROWS_DEV), jax.random.fold_in(splits[7], 1), 0, ROWS_DEV - 1).astype(jnp.int32),
        "freq": jnp.clip(jnp.exp(jax.random.uniform(splits[8], (TD,), jnp.float32, math.log(0.001), math.log(0.5))), 0.001, 0.5),
        "phase": jnp.clip(jax.random.uniform(splits[9], (TD,), jnp.float32, -3.140625, 3.140625), -3.140625, 3.140625),
        "w_query": gaussian(splits[10], (W + TD, W), (W + TD) ** -0.5, 0.25, ((1, 2),)),
        "w_key": gaussian(splits[11], (W + TD, W), (W + TD) ** -0.5, 0.25, ((1, 2),)),
        "w_value": gaussian(splits[12], (W + TD, W), (W + TD) ** -0.5, 0.25, ((1, 2),)),
        "w_out": gaussian(splits[13], (W, W), W ** -0.5, 0.25, ((0, 2),)),
        "w_self": gaussian(splits[14], (W, W), W ** -0.5, 0.25, ((0, 2),)),
        "w_msg_self": gaussian(splits[15], (W, MSG), W ** -0.5, 0.25, ((0, 2),)),
        "w_msg_other": gaussian(splits[16], (W, MSG), W ** -0.5, 0.25, ((0, 2),)),
        "w_msg_time": gaussian(splits[17], (TD, MSG), TD ** -0.5, 0.5, ((0, 2),)),
        "w_msg_edge": gaussian(splits[18], (EF, MSG), EF ** -0.5, 0.5, ((0, 2),)),
        "w_in": gaussian(splits[19], (MSG, 3, W), MSG ** -0.5, 0.25, ((2, 2),)),
        "w_hid": gaussian(splits[20], (W, 3, W), W ** -0.5, 0.25, ((2, 2),)),
    }


def encode(delta, freq, phase):
    return jnp.cos(delta.astype(jnp.float32)[..., None] * freq + phase)

def reference(memory, ev_time, nbr_time, edge_feat, self_slot, nbr_slot, serve_self, serve_rows, freq, phase, w_query, w_key, w_value, w_out, w_self, w_msg_self, w_msg_other, w_msg_time, w_msg_edge, w_in, w_hid):
    owner_base = (jnp.arange(PEERS, dtype=jnp.int32) * ROWS_DEV)[:, None, None]
    nbr_table = jnp.transpose(owner_base + serve_rows.astype(jnp.int32), (1, 0, 2)).reshape(PEERS, PEERS * CAP)
    self_table = jnp.transpose(owner_base + serve_self.astype(jnp.int32), (1, 0, 2)).reshape(PEERS, PEERS * CAP_SELF)
    te_self = jnp.cos(phase).astype(jnp.bfloat16)[None]

    def block(args):
        self_look, nbr_look, times, nbr_times, edges, ntab, stab = args
        self_rows = stab[self_look]
        nbr_rows = ntab[nbr_look]
        self_mem = memory[self_rows].reshape(-1, W)
        nbrs = memory[nbr_rows].reshape(-1, W)
        other = memory[self_rows[:, ::-1]].reshape(-1, W)
        te_nbr = encode(times[:, None, None] - nbr_times, freq, phase).astype(jnp.bfloat16).reshape(-1, TD)
        query = (jnp.dot(self_mem, w_query[:W], preferred_element_type=jnp.float32) + jnp.dot(te_self, w_query[W:], preferred_element_type=jnp.float32)).astype(jnp.bfloat16)
        keys = (jnp.dot(nbrs, w_key[:W], preferred_element_type=jnp.float32) + jnp.dot(te_nbr, w_key[W:], preferred_element_type=jnp.float32)).astype(jnp.bfloat16)
        values = (jnp.dot(nbrs, w_value[:W], preferred_element_type=jnp.float32) + jnp.dot(te_nbr, w_value[W:], preferred_element_type=jnp.float32)).astype(jnp.bfloat16)
        qh = query.reshape(-1, HEADS, HEAD).astype(jnp.float32)
        kh = keys.reshape(-1, K, HEADS, HEAD).astype(jnp.float32)
        vh = values.reshape(-1, K, HEADS, HEAD).astype(jnp.float32)
        score = jnp.einsum('nhd,nkhd->nhk', qh, kh) / jnp.sqrt(jnp.float32(HEAD))
        expo = jnp.exp(score)
        weights = (expo / lax.optimization_barrier(jnp.sum(expo, axis=-1, keepdims=True))).astype(jnp.bfloat16)
        att = jnp.einsum('nhk,nkhd->nhd', weights.astype(jnp.float32), vh).astype(jnp.bfloat16).reshape(-1, W)
        emb = (jnp.dot(att, w_out, preferred_element_type=jnp.float32) + jnp.dot(self_mem, w_self, preferred_element_type=jnp.float32)).astype(jnp.bfloat16)
        te_msg = encode(times[:, None] - nbr_times[:, :, 0], freq, phase).astype(jnp.bfloat16).reshape(-1, TD)
        edge_two = jnp.broadcast_to(edges[:, None], (edges.shape[0], 2, EF)).reshape(-1, EF)
        msg = jnp.dot(self_mem, w_msg_self, preferred_element_type=jnp.float32) + jnp.dot(other, w_msg_other, preferred_element_type=jnp.float32) + jnp.dot(te_msg, w_msg_time, preferred_element_type=jnp.float32) + jnp.dot(edge_two, w_msg_edge, preferred_element_type=jnp.float32)
        return (emb.reshape(-1, 2, W), msg, self_rows.reshape(-1))
    embedding, msg, dest = lax.map(block, (self_slot.reshape(PEERS, EV_DEV, 2), nbr_slot.reshape(PEERS, EV_DEV, 2, K), ev_time.reshape(PEERS, EV_DEV), nbr_time.reshape(PEERS, EV_DEV, 2, K), edge_feat.reshape(PEERS, EV_DEV, EF), nbr_table, self_table))
    embedding = embedding.reshape(EVENTS, 2, W)
    total = jnp.zeros((NODES, MSG), jnp.float32).at[dest.reshape(-1)].add(msg.reshape(-1, MSG))
    count = jnp.zeros((NODES,), jnp.float32).at[dest.reshape(-1)].add(jnp.ones((dest.size,), jnp.float32))

    def update(args):
        tot, cnt, state = args
        mean = (tot / jnp.maximum(cnt, 1.0)[:, None]).astype(jnp.bfloat16)
        gi = jnp.dot(mean, w_in.reshape(MSG, 3 * W), preferred_element_type=jnp.float32).reshape(-1, 3, W)
        gh = jnp.dot(state, w_hid.reshape(W, 3 * W), preferred_element_type=jnp.float32).reshape(-1, 3, W)
        reset = jax.nn.sigmoid(gi[:, 0] + gh[:, 0])
        gate = jax.nn.sigmoid(gi[:, 1] + gh[:, 1])
        cand = jnp.tanh(gi[:, 2] + reset * gh[:, 2])
        old = state.astype(jnp.float32)
        fresh = (1.0 - gate) * cand + gate * old
        return jnp.where(cnt[:, None] > 0, fresh, old).astype(jnp.bfloat16)
    memory_out = lax.map(update, (total.reshape(PEERS, ROWS_DEV, MSG), count.reshape(PEERS, ROWS_DEV), memory.reshape(PEERS, ROWS_DEV, W))).reshape(NODES, W)
    return (embedding, memory_out)
```

```python
import functools

import jax
import jax.numpy as jnp
from jax import lax
from jax.experimental import pallas as pl
from jax.experimental.pallas import tpu as pltpu
from jax.sharding import PartitionSpec as P

HEADS = 8
GROUP = 16
BF = jnp.bfloat16
F32 = jnp.float32
I32 = jnp.int32
VMEM = pl.BlockSpec(memory_space=pltpu.VMEM)
TURN = 6.283185307179586
COS = (
    6.52861337,
    -25.9675685,
    60.1676231,
    -85.4501386,
    64.9391174,
    -19.7392045,
    0.999999989,
)


def dot(a, b):
    return jnp.dot(a, b, preferred_element_type=F32)


def dot_nt(a, b):
    return lax.dot_general(a, b, (((1,), (1,)), ((), ())), preferred_element_type=F32)


def iota(shape, dim):
    return lax.broadcasted_iota(I32, shape, dim)


def one_hot(mask):
    return jnp.where(mask, 1.0, 0.0).astype(BF)


def params():
    return pltpu.CompilerParams(vmem_limit_bytes=48 * 1024 * 1024)


def cost(flops, size):
    return pl.CostEstimate(flops=int(flops), bytes_accessed=int(size), transcendentals=0)


def split(serve):
    high = lax.shift_right_logical(serve, 8)
    low = jnp.bitwise_and(serve, 255)
    return high.astype(F32).astype(BF), low.astype(F32).astype(BF)


def column(serve, start, count):
    peers, cap = serve.shape
    high, low = split(serve)
    pick = one_hot((iota((count, peers), 0) + start) // cap == iota((count, peers), 1))
    every = 256.0 * dot(pick, high) + dot(pick, low)
    mine = (iota((count, cap), 0) + start) % cap == iota((count, cap), 1)
    return jnp.sum(jnp.where(mine, every, 0.0), axis=1, keepdims=True)


def row(serve):
    peers, cap = serve.shape
    slots = peers * cap
    high, low = split(serve)
    pick = one_hot(iota((cap, slots), 1) % cap == iota((cap, slots), 0))
    every = 256.0 * dot(high, pick) + dot(low, pick)
    mine = iota((peers, slots), 1) // cap == iota((peers, slots), 0)
    return jnp.sum(jnp.where(mine, every, 0.0), axis=0, keepdims=True)


def rows_at(col, count):
    at = iota((col.shape[0], count), 1).astype(F32)
    return one_hot(at == col)


def half_of(core, half):
    return pl.ds(pl.multiple_of(core * half, half), half)


def serve_kernel(packed, rows_ref, self_ref, mem_ref, *outs):
    core = lax.axis_index("mp")
    count, width = mem_ref.shape
    half = width // 2
    mem = mem_ref[:, half_of(core, half)]
    done = 0
    for table, (ref, out) in enumerate(((rows_ref, outs[0]), (self_ref, outs[-1]))):
        serve = ref[0]
        peers, cap = serve.shape
        slots = peers * cap
        step = min(256, slots)
        for start in range(0, slots, step):
            picked = dot(rows_at(column(serve, start, step), count), mem).astype(BF)
            if packed:
                out[start // cap : (start + step) // cap, done : done + cap, :] = picked.reshape(
                    step // cap, cap, half
                )
            else:
                out[start : start + step, :] = picked
        done += cap


def encode_turns(x):
    turns = x * (1.0 / TURN)
    u = turns - jnp.round(turns)
    square = u * u
    total = jnp.full_like(square, COS[0])
    for factor in COS[1:]:
        total = total * square + factor
    return total


def grouped_column(block):
    return jnp.concatenate([block[:, k : k + 1] for k in range(block.shape[1])], axis=0)


def time_kernel(delta_ref, freq_ref, phase_ref, te_ref, msg_ref):
    ends, neigh = delta_ref.shape
    size = GROUP * neigh
    freq = freq_ref[...]
    phase = phase_ref[...]

    def body(g, carry):
        at = pl.ds(pl.multiple_of(g * GROUP, GROUP), GROUP)
        col = grouped_column(delta_ref[at, :])
        enc = encode_turns(col * freq + phase).astype(BF)
        te_ref[pl.ds(pl.multiple_of(g * size, size), size), :] = enc
        msg_ref[at, :] = enc[:GROUP, :]
        return carry

    lax.fori_loop(0, ends // GROUP, body, 0)


def slot_kernel(
    peers,
    slot_ref,
    slot_t_ref,
    te_ref,
    edge_ref,
    edge_x_ref,
    wt_ref,
    we_ref,
    wx_ref,
    pairs_ref,
    count_ref,
    sent_ref,
    pre_ref,
):
    core = lax.axis_index("mp")
    events = slot_ref.shape[0]
    slots, half = pre_ref.shape
    cap = slots // peers
    part = wt_ref.shape[0]
    tall = [one_hot(iota((slots, events), 0) == slot_t_ref[j : j + 1, :]) for j in range(2)]
    wide = [one_hot(iota((events, slots), 1) == slot_ref[:, j : j + 1]) for j in range(2)]
    pairs_ref[...] = (dot(tall[0], wide[1]) + dot(tall[1], wide[0])).astype(BF)
    ones = jnp.ones((events, 128), BF)
    count_ref[...] = dot(tall[0], ones) + dot(tall[1], ones)
    lane = iota((slots, 128), 1)
    place = one_hot(iota((slots, 128), 0) % cap == lane)
    spread = (count_ref[...] * place.astype(F32)).astype(BF)
    owner = one_hot(iota((peers, slots), 1) // cap == iota((peers, slots), 0))
    sent_ref[...] = dot(owner, spread)
    cols = half_of(core, half)
    wx = wx_ref[wx_ref.shape[0] - 2 * part :, cols]
    mine, theirs = wt_ref[:, cols], wx[:part]
    first = core == 0
    w_time = jnp.concatenate(
        [jnp.where(first, mine, theirs), jnp.where(first, theirs, mine)], axis=0
    )
    edge = dot(edge_ref[...], we_ref[:, cols]) + dot(edge_x_ref[...], wx[part:])
    total = jnp.zeros((slots, half), F32)
    for j in range(2):
        value = dot(te_ref[j * events : (j + 1) * events, :], w_time) + edge
        high = value.astype(BF)
        low = (value - high.astype(F32)).astype(BF)
        total = total + dot(tall[j], high) + dot(tall[j], low)
    pre_ref[...] = total


def owner_kernel(self_ref, mem_ref, whid_ref, gh_ref, same_ref, put_ref, base_ref):
    core = lax.axis_index("mp")
    count, width = mem_ref.shape
    half = width // 2
    serve = self_ref[0]
    slots = serve.size
    for start in range(0, slots, 256):
        picked = dot(rows_at(column(serve, start, 256), count), mem_ref[...]).astype(BF)
        gh_ref[start : start + 256, :] = dot(picked, whid_ref[...])
    col = column(serve, 0, slots)
    line = row(serve)
    same = col == line
    same_ref[...] = one_hot(same)
    earlier = same & (iota((slots, slots), 0) < iota((slots, slots), 1))
    again = jnp.sum(jnp.where(earlier, 1.0, 0.0), axis=0, keepdims=True)
    line = jnp.where(again > 0, -1.0, line)
    step = 256
    for start in range(0, count, step):
        at = (iota((step, slots), 0) + start).astype(F32)
        hit = jnp.where(at == line, 1.0, 0.0)
        put_ref[start : start + step, :] = hit.astype(BF)
        free = 1.0 - jnp.sum(hit, axis=1, keepdims=True)
        old = mem_ref[start : start + step, half_of(core, half)].astype(F32)
        base_ref[start : start + step, :] = (old * free).astype(BF)


def part_of(ref, packed, start, size):
    if packed:
        return ref[:, start : start + size, :].reshape(-1, ref.shape[2])
    return ref[...]


def message_kernel(
    packed,
    cap,
    cap_self,
    own_ref,
    oth_ref,
    ws_ref,
    wo_ref,
    wx_ref,
    pairs_ref,
    count_ref,
    sent_ref,
    pre_ref,
    out_ref,
):
    core = lax.axis_index("mp")
    half = ws_ref.shape[0]
    cols = half_of(core, half)
    own = part_of(own_ref, packed, cap, cap_self)
    oth = part_of(oth_ref, packed, cap, cap_self)
    other = dot(own, wo_ref[:, cols]) + dot(oth, wx_ref[half : 2 * half, cols])
    mine = dot(own, ws_ref[:, cols]) + dot(oth, wx_ref[:half, cols])
    count = jnp.concatenate([count_ref[...]] * (half // 128), axis=1)
    total = dot(pairs_ref[...], other.astype(BF)) + count * mine + pre_ref[...]
    out = total.astype(BF)
    if not packed:
        out_ref[...] = out
        return
    peers = out.shape[0] // cap_self
    tiles = half // 128
    for tile in range(tiles):
        out_ref[:, tile * cap_self : (tile + 1) * cap_self, :] = out[
            :, tile * 128 : (tile + 1) * 128
        ].reshape(peers, cap_self, 128)
    sent = sent_ref[...]
    out_ref[:, tiles * cap_self :, :] = jnp.broadcast_to(sent[:, None, :], (peers, 16, 128)).astype(
        BF
    )


def attention_kernel(
    packed,
    cap,
    cap_self,
    nown_ref,
    noth_ref,
    sown_ref,
    soth_ref,
    slot_ref,
    nslot_ref,
    te_ref,
    phase_ref,
    wq_ref,
    wk_ref,
    wv_ref,
    wout_ref,
    wself_ref,
    emb_ref,
    kv_w,
    att_ref,
):
    core = lax.axis_index("mp")
    half = wout_ref.shape[0]
    width = 2 * half
    mine, theirs = half_of(core, half), half_of(1 - core, half)
    fown = part_of(nown_ref, packed, 0, cap)
    foth = part_of(noth_ref, packed, 0, cap)
    slots = fown.shape[0]
    for place, ref in enumerate((wk_ref, wv_ref)):
        cols = slice(place * half, (place + 1) * half)
        kv_w[:slots, cols] = (dot(fown, ref[mine, :]) + dot(foth, ref[theirs, :])).astype(BF)
        kv_w[slots:, cols] = ref[width:, :]
    xown = part_of(sown_ref, packed, cap, cap_self)
    xoth = part_of(soth_ref, packed, cap, cap_self)
    te_self = encode_turns(phase_ref[...]).astype(BF)
    te_self = jnp.broadcast_to(te_self, (16, te_self.shape[1]))
    query = dot(xown, wq_ref[mine, :]) + dot(xoth, wq_ref[theirs, :])
    query = (query + dot(te_self, wq_ref[width:, :])[:1]).astype(BF)
    ends, neigh = nslot_ref.shape
    events = ends // 2
    at = iota((events, xown.shape[0]), 1)
    find = jnp.concatenate([one_hot(at == slot_ref[:, j : j + 1]) for j in range(2)], axis=0)
    q = (dot(find, query) * (1.0 / (width // HEADS) ** 0.5)).astype(BF)
    heads = HEADS // 2
    size = width // HEADS
    tall = heads * GROUP
    pick = iota((tall, half), 1) // size == iota((tall, half), 0) // GROUP
    pairs = GROUP * neigh
    member = iota((tall, pairs), 1) % GROUP == iota((tall, pairs), 0) % GROUP
    lanes = iota((pairs, slots), 1)
    att_ref[...] = q

    def body(g, carry):
        at = pl.ds(pl.multiple_of(g * GROUP, GROUP), GROUP)
        col = grouped_column(nslot_ref[at, :])
        te = te_ref[pl.ds(pl.multiple_of(g * pairs, pairs), pairs), :]
        left = jnp.concatenate([one_hot(lanes == col), te], axis=1)
        kv = dot(left, kv_w[...]).astype(BF)
        q4 = jnp.concatenate([att_ref[at, :]] * heads, axis=0)
        q4 = jnp.where(pick, q4, jnp.zeros_like(q4))
        score = dot_nt(q4, kv[:, :half])
        expo = jnp.where(member, jnp.exp(score), 0.0)
        weights = (expo / jnp.sum(expo, axis=1, keepdims=True)).astype(BF)
        mixed = jnp.where(pick, dot(weights, kv[:, half:]), 0.0)
        att = sum(mixed[h * GROUP : (h + 1) * GROUP] for h in range(heads))
        att_ref[at, :] = att.astype(BF)
        return carry

    lax.fori_loop(0, ends // GROUP, body, 0)
    self_own = dot(find, xown).astype(BF)
    emb_ref[...] = dot(att_ref[...], wout_ref[...]) + dot(self_own, wself_ref[...])


def update_kernel(
    packed,
    cap_self,
    own_ref,
    oth_ref,
    cnt_ref,
    same_ref,
    win_ref,
    gh_ref,
    old_ref,
    put_ref,
    base_ref,
    out_ref,
):
    core = lax.axis_index("mp")
    half = base_ref.shape[1]
    slots = same_ref.shape[0]
    tiles = half // 128

    def messages(ref):
        if not packed:
            return ref[...]
        return jnp.concatenate(
            [
                ref[:, tile * cap_self : (tile + 1) * cap_self, :].reshape(slots, 128)
                for tile in range(tiles)
            ],
            axis=1,
        )

    peers = slots // cap_self
    counts = cnt_ref[:, tiles * cap_self :, :][:, 0, :] if packed else cnt_ref[...]
    spread = dot(one_hot(iota((slots, peers), 0) // cap_self == iota((slots, peers), 1)), counts)
    lane = iota((slots, 128), 1)
    spread = jnp.where(iota((slots, 128), 0) % cap_self == lane, spread, 0.0).astype(BF)
    same = same_ref[...]
    count = jnp.sum(dot(same, spread), axis=1, keepdims=True)
    inverse = 1.0 / jnp.maximum(count, 1.0)
    own = (dot(same, messages(own_ref)) * inverse).astype(BF)
    oth = (dot(same, messages(oth_ref)) * inverse).astype(BF)
    gi = dot(own, win_ref[half_of(core, half), :]) + dot(oth, win_ref[half_of(1 - core, half), :])
    gh = gh_ref[...]
    reset = jax.nn.sigmoid(gi[:, :half] + gh[:, :half])
    gate = jax.nn.sigmoid(gi[:, half : 2 * half] + gh[:, half : 2 * half])
    cand = jnp.tanh(gi[:, 2 * half :] + reset * gh[:, 2 * half :])
    old = old_ref[:, old_ref.shape[1] - cap_self :, :].reshape(slots, half) if packed else old_ref[...]
    old = old.astype(F32)
    fresh = jnp.where(count > 0, (1.0 - gate) * cand + gate * old, old).astype(BF)
    step = 256
    for start in range(0, base_ref.shape[0], step):
        at = slice(start, start + step)
        put = dot(put_ref[at, :], fresh)
        out_ref[at, :] = (base_ref[at, :].astype(F32) + put).astype(BF)


def per_device(
    memory,
    ev_time,
    nbr_time,
    edge_feat,
    self_slot,
    nbr_slot,
    serve_self,
    serve_rows,
    freq,
    phase,
    w_query,
    w_key,
    w_value,
    w_out,
    w_self,
    w_msg_self,
    w_msg_other,
    w_msg_time,
    w_msg_edge,
    w_in,
    w_hid,
):
    owned, width = memory.shape
    half = w_out.shape[0]
    peers, cap = serve_rows.shape[1:]
    cap_self = serve_self.shape[2]
    events, _, neigh = nbr_slot.shape
    ends = 2 * events
    tdim = freq.shape[0]
    slots_n, slots_s = peers * cap, peers * cap_self
    packed = cap % 16 == 0 and cap_self % 16 == 0
    shape = jax.ShapeDtypeStruct

    def call(kernel, out_shape, args, flops=0, scratch=()):
        outs = out_shape if isinstance(out_shape, (list, tuple)) else [out_shape]
        size = sum(a.size * a.dtype.itemsize for a in (*args, *outs))
        return pl.pallas_call(
            kernel,
            out_shape=out_shape,
            in_specs=[VMEM] * len(args),
            out_specs=jax.tree.map(lambda _: VMEM, out_shape),
            scratch_shapes=list(scratch),
            compiler_params=params(),
            cost_estimate=cost(flops, size),
        )(*args)

    def swap(x):
        return lax.ppermute(x, "mp", [(0, 1), (1, 0)])

    def exchange(x):
        return lax.all_to_all(x, "nodes", split_axis=0, concat_axis=0, tiled=True)

    flops_serve = 2 * (slots_n + slots_s) * owned * half
    if packed:
        served = call(
            functools.partial(serve_kernel, True),
            shape((peers, cap + cap_self, half), BF),
            (serve_rows, serve_self, memory),
            flops_serve,
        )
        old = served
    else:
        served_n, old = call(
            functools.partial(serve_kernel, False),
            [shape((slots_n, half), BF), shape((slots_s, half), BF)],
            (serve_rows, serve_self, memory),
            flops_serve,
        )
        served = jnp.concatenate(
            [served_n.reshape(peers, cap, half), old.reshape(peers, cap_self, half)], axis=1
        )
    fetched = exchange(served)

    w_swap = swap(jnp.concatenate([w_msg_self, w_msg_other, w_msg_time, w_msg_edge], axis=0))
    edge_swap = swap(edge_feat)
    slot_t = self_slot.T
    delta = (ev_time[:, None, None] - nbr_time).astype(F32).transpose(1, 0, 2).reshape(ends, neigh)
    nslot = nbr_slot.transpose(1, 0, 2).reshape(ends, neigh)
    te, te_msg = call(
        time_kernel,
        [shape((ends * neigh, tdim), BF), shape((ends, tdim), BF)],
        (delta, freq[None], phase[None]),
        ends * neigh * tdim * 40,
    )
    pairs, count, sent, pre = call(
        functools.partial(slot_kernel, peers),
        [
            shape((slots_s, slots_s), BF),
            shape((slots_s, 128), F32),
            shape((peers, 128), F32),
            shape((slots_s, half), F32),
        ],
        (
            self_slot,
            slot_t,
            te_msg,
            edge_feat,
            edge_swap,
            w_msg_time,
            w_msg_edge,
            w_swap,
        ),
        4 * slots_s * events * (slots_s + half),
    )
    gh, same, put, base = call(
        owner_kernel,
        [
            shape((slots_s, 3 * half), F32),
            shape((slots_s, slots_s), BF),
            shape((owned, slots_s), BF),
            shape((owned, half), BF),
        ],
        (serve_self, memory, w_hid.reshape(width, 3 * half)),
        2 * slots_s * (owned * width + width * 3 * half),
    )

    fetched_x = swap(fetched)
    if packed:
        nown = sown = fetched
        noth = soth = fetched_x
        back_shape = shape((peers, (half // 128) * cap_self + 16, 128), BF)
    else:
        nown, noth = (f[:, :cap].reshape(slots_n, half) for f in (fetched, fetched_x))
        sown, soth = (f[:, cap:].reshape(slots_s, half) for f in (fetched, fetched_x))
        back_shape = shape((slots_s, half), BF)
    message = call(
        functools.partial(message_kernel, packed, cap, cap_self),
        back_shape,
        (sown, soth, w_msg_self, w_msg_other, w_swap, pairs, count, sent, pre),
        2 * slots_s * half * (2 * width + slots_s),
    )
    if packed:
        back = exchange(message)
        counts = back
        back_x = swap(back)
    else:
        message = jnp.concatenate(
            [
                message.reshape(peers, cap_self, half),
                jnp.pad(sent.astype(BF), ((0, 0), (0, half - 128)))[:, None],
            ],
            axis=1,
        )
        back = exchange(message)
        back_x = swap(back)[:, :cap_self].reshape(slots_s, half)
        counts = back[:, cap_self, :128]
        back = back[:, :cap_self].reshape(slots_s, half)

    part = call(
        functools.partial(attention_kernel, packed, cap, cap_self),
        shape((ends, width), F32),
        (
            nown,
            noth,
            sown,
            soth,
            self_slot,
            nslot,
            te,
            phase[None],
            w_query,
            w_key,
            w_value,
            w_out,
            w_self,
        ),
        2 * ends * neigh * (slots_n + tdim) * width,
        [pltpu.VMEM((slots_n + tdim, 2 * half), BF), pltpu.VMEM((ends, half), BF)],
    )
    embedding = (part + swap(part)).astype(BF).reshape(2, events, width).transpose(1, 0, 2)

    memory_out = call(
        functools.partial(update_kernel, packed, cap_self),
        shape((owned, half), BF),
        (back, back_x, counts, same, w_in.reshape(width, 3 * half), gh, old, put, base),
        2 * slots_s * (slots_s * width + width * 3 * half + owned * half),
    )
    return (embedding, memory_out)


def solution(mesh):
    return jax.shard_map(
        per_device,
        mesh=mesh,
        in_specs=(
            P("nodes", None),
            P("nodes"),
            P("nodes", None, None),
            P("nodes", "mp"),
            P("nodes", None),
            P("nodes", None, None),
            P("nodes", None, None),
            P("nodes", None, None),
            P(),
            P(),
            P(None, "mp"),
            P(None, "mp"),
            P(None, "mp"),
            P("mp", None),
            P("mp", None),
            P("mp", None),
            P("mp", None),
            P("mp", None),
            P("mp", None),
            P(None, None, "mp"),
            P(None, None, "mp"),
        ),
        out_specs=(P("nodes", None, None), P("nodes", "mp")),
        check_vma=False,
    )
```

```python
import functools

import jax
import jax.numpy as jnp
from jax import lax
from jax.experimental import pallas as pl
from jax.experimental.pallas import tpu as pltpu
from jax.sharding import PartitionSpec as P

HEADS = 8
BF = jnp.bfloat16
F32 = jnp.float32
I32 = jnp.int32
VMEM = pl.BlockSpec(memory_space=pltpu.VMEM)
HBM = pl.BlockSpec(memory_space=pltpu.HBM)
TURN = 6.283185307179586
COS = (
    6.52861337,
    -25.9675685,
    60.1676231,
    -85.4501386,
    64.9391174,
    -19.7392045,
    0.999999989,
)


def dot(a, b):
    return jnp.dot(a, b, preferred_element_type=F32)


def dot_nt(a, b):
    return lax.dot_general(a, b, (((1,), (1,)), ((), ())), preferred_element_type=F32)


def iota(shape, dim):
    return lax.broadcasted_iota(I32, shape, dim)


class Operand:
    def __init__(self, copy, ref):
        self.copy, self.ref, self.shape = copy, ref, ref.shape
        copy.start()

    def wait(self):
        if self.copy is not None:
            self.copy.wait()
            self.copy = None

    def __getitem__(self, at):
        self.wait()
        return self.ref[at]


class Result:
    def __init__(self, room, ref, sems, parts):
        self.room, self.ref, self.sems, self.parts = room, ref, sems, parts
        self.shape, self.sent = room.shape, []

    def __setitem__(self, at, value):
        self.room[at] = value

    def __getitem__(self, at):
        return self.room[at]

    def send(self, part):
        size = self.shape[0] // self.parts
        at = pl.ds(part * size, size)
        copy = pltpu.make_async_copy(self.room.at[at], self.ref.at[at], self.sems.at[part])
        copy.start()
        self.sent.append((part, copy))

    def finish(self):
        done = [part for part, _ in self.sent]
        for part in range(self.parts):
            if part not in done:
                self.send(part)
        for _, copy in self.sent:
            copy.wait()


def staged(kernel, views, parts, *refs):
    count, outs = len(views), len(parts)
    ins, results, rest = refs[:count], refs[count : count + outs], list(refs[count + outs :])
    in_sems, out_sems = rest[-2:]
    rest = rest[:-2]
    operands = []
    for n, (ref, view) in enumerate(zip(ins, views)):
        if view is None:
            operands.append(ref)
        else:
            room = rest.pop(0)
            operands.append(Operand(pltpu.make_async_copy(view(ref), room, in_sems.at[n]), room))
    held = [
        Result(rest.pop(0), ref, out_sems.at[n], part)
        for n, (ref, part) in enumerate(zip(results, parts))
    ]
    kernel(*operands, *held, *rest)
    for operand in operands:
        if isinstance(operand, Operand):
            operand.wait()
    for result in held:
        result.finish()


def one_hot(mask):
    return jnp.where(mask, 1.0, 0.0).astype(BF)


def split(serve):
    high = lax.shift_right_logical(serve, 8)
    low = jnp.bitwise_and(serve, 255)
    return high.astype(F32).astype(BF), low.astype(F32).astype(BF)


def column(serve, start, count):
    peers, cap = serve.shape
    high, low = split(serve)
    pick = one_hot((iota((count, peers), 0) + start) // cap == iota((count, peers), 1))
    every = 256.0 * dot(pick, high) + dot(pick, low)
    mine = (iota((count, cap), 0) + start) % cap == iota((count, cap), 1)
    return jnp.sum(jnp.where(mine, every, 0.0), axis=1, keepdims=True)


def row(serve):
    peers, cap = serve.shape
    slots = peers * cap
    high, low = split(serve)
    pick = one_hot(iota((cap, slots), 1) % cap == iota((cap, slots), 0))
    every = 256.0 * dot(high, pick) + dot(low, pick)
    mine = iota((peers, slots), 1) // cap == iota((peers, slots), 0)
    return jnp.sum(jnp.where(mine, every, 0.0), axis=0, keepdims=True)


def rows_at(col, count):
    at = iota((col.shape[0], count), 1).astype(F32)
    return one_hot(at == col)


def half_of(core, half):
    return pl.ds(pl.multiple_of(core * half, half), half)


def serve_kernel(packed, rows_ref, self_ref, *refs):
    mems, outs, hot = refs[:4], refs[4:-1], refs[-1]
    depth, half = mems[0].shape
    count = len(mems) * depth
    step = 256
    rows, own = rows_ref[0], self_ref[0]
    jobs = []
    for table, serve in enumerate((rows, own)):
        jobs += [(start, table, serve) for start in range(0, serve.size, step)]
    jobs.sort(key=lambda job: (job[0], job[1]))
    early = hot.shape[0] // step
    for n, (start, table, serve) in enumerate(jobs[:early]):
        hot[n * step : (n + 1) * step, :] = rows_at(column(serve, start, step), count)
    for n, (start, table, serve) in enumerate(jobs):
        if n < early:
            at = hot[n * step : (n + 1) * step, :]
        else:
            at = rows_at(column(serve, start, step), count)
        picked = dot(at[:, :depth], mems[0][...])
        for part in range(1, len(mems)):
            picked = picked + dot(at[:, part * depth : (part + 1) * depth], mems[part][...])
        picked = picked.astype(BF)
        if packed:
            cap = serve.shape[1]
            first = table * rows.shape[1]
            outs[0][start // cap : (start + step) // cap, first : first + cap, :] = picked.reshape(
                step // cap, cap, half
            )
            if outs[0].parts > 1 and table == 1:
                outs[0].send(start // step)
        else:
            outs[table][start : start + step, :] = picked


def encode_turns(x):
    turns = x * (1.0 / TURN)
    u = turns - jnp.round(turns)
    square = u * u
    total = jnp.full_like(square, COS[0])
    for factor in COS[1:]:
        total = total * square + factor
    return total


def down(line, count):
    return jnp.broadcast_to(line, (count, line.shape[1])).T


def time_kernel(ev_ref, nbr_ref, freq_ref, phase_ref, wq_ref, wk_ref, wv_ref, te_ref, wqt_ref, wkvt_ref):
    neigh, tdim, ends = te_ref.shape
    events = ends // 2
    freq = down(freq_ref[...], events)
    phase = down(phase_ref[...], events)
    time = ev_ref[...]
    for k in range(neigh):
        for j in range(2):
            delta = (time - nbr_ref[j, k : k + 1, :]).astype(F32)
            enc = encode_turns(delta * freq + phase)
            te_ref[k, :, j * events : (j + 1) * events] = enc.astype(BF)
    half = wq_ref.shape[1]
    wqt_ref[...] = wq_ref[...].T
    wkvt_ref[:half, :] = wk_ref[...].T
    wkvt_ref[half:, :] = wv_ref[...].T


def tall_one_hot(slot_t_ref, slots):
    events = slot_t_ref.shape[1]
    at = iota((slots, events), 0)
    return [one_hot(at == slot_t_ref[j : j + 1, :]) for j in range(2)]


def pack_places(slots, half):
    at_pre = slots + 128
    at_weight = at_pre + 2 * half
    at_sent = at_weight + 2 * half
    return slots, at_pre, at_weight, at_sent, at_sent + 128


def slot_kernel(
    peers,
    slot_t_ref,
    te_ref,
    edge_ref,
    edge_x_ref,
    wt_ref,
    we_ref,
    ws_ref,
    wo_ref,
    wx_ref,
    pack_ref,
):
    core = lax.axis_index("mp")
    slots = pack_ref.shape[0]
    part, half = wt_ref.shape
    tall = tall_one_hot(slot_t_ref, slots)
    events = tall[0].shape[1]
    both = tall[0] + tall[1]
    at_count, at_pre, at_weight, at_sent = pack_places(slots, half)[:4]
    pack_ref[:, :at_count] = (dot_nt(tall[0], tall[1]) + dot_nt(tall[1], tall[0])).astype(BF)
    count = dot_nt(both, jnp.ones((128, events), BF))
    pack_ref[:, at_count:at_pre] = count.astype(BF)
    cap = slots // peers
    place = iota((slots, 128), 0) % cap == iota((slots, 128), 1)
    owner = one_hot(iota((peers, slots), 1) // cap == iota((peers, slots), 0))
    pack_ref[:peers, at_sent:] = dot(owner, jnp.where(place, count, 0.0).astype(BF)).astype(BF)
    pack_ref[peers:, at_sent:] = jnp.zeros((slots - peers, 128), BF)
    pack_ref[:half, at_weight : at_weight + half] = wo_ref[...]
    pack_ref[:half, at_weight + half : at_sent] = ws_ref[...]
    pack_ref[half : 2 * half, at_weight : at_weight + half] = wx_ref[half : 2 * half, :]
    pack_ref[half : 2 * half, at_weight + half : at_sent] = wx_ref[:half, :]
    mine, theirs = wt_ref[...], wx_ref[2 * half : 2 * half + part, :]
    first = core == 0
    weight = jnp.concatenate(
        [
            jnp.where(first, mine, theirs),
            jnp.where(first, theirs, mine),
            we_ref[...],
            wx_ref[2 * half + part :, :],
        ],
        axis=0,
    )
    edge = jnp.concatenate([edge_ref[...], edge_x_ref[...]], axis=0)
    value = jnp.concatenate(
        [dot_nt(jnp.concatenate(tall, axis=1), te_ref[0]), dot_nt(both, edge)], axis=1
    )
    high = value.astype(BF)
    low = (value - high.astype(F32)).astype(BF)
    pre = dot(high, weight) + dot(low, weight)
    high = pre.astype(BF)
    pack_ref[:, at_pre : at_pre + half] = high
    pack_ref[:, at_pre + half : at_weight] = (pre - high.astype(F32)).astype(BF)


def prepare_kernel(
    self_ref,
    ev_ref,
    nbr_ref,
    freq_ref,
    phase_ref,
    mem_ref,
    whid_ref,
    wq_ref,
    wk_ref,
    wv_ref,
    gh_ref,
    te_ref,
    wqt_ref,
    wkvt_ref,
):
    time_kernel(ev_ref, nbr_ref, freq_ref, phase_ref, wq_ref, wk_ref, wv_ref, te_ref, wqt_ref, wkvt_ref)
    te_ref.send(0)
    wqt_ref.send(0)
    wkvt_ref.send(0)
    count, width = mem_ref.shape
    serve = self_ref[0]
    slots = serve.size
    col = column(serve, 0, slots)
    for start in range(0, slots, 256):
        at = slice(start, start + 256)
        picked = dot(rows_at(col[at], count), mem_ref[...]).astype(BF)
        for g in range(3):
            gh_ref[g, at, :] = dot(picked, whid_ref[g])


def place_kernel(self_ref, mem_ref, base_ref):
    count, half = mem_ref.shape
    serve = self_ref[0]
    line = row(serve)
    step = count // base_ref.parts
    for part in range(base_ref.parts):
        at = slice(part * step, (part + 1) * step)
        hit = (iota((step, serve.size), 0) + part * step).astype(F32) == line
        served = jnp.max(jnp.where(hit, 1.0, 0.0), axis=1, keepdims=True)
        base_ref[at, :] = (mem_ref[at, :].astype(F32) * (1.0 - served)).astype(BF)
        base_ref.send(part)


def part_of(ref, packed, start, size):
    if packed:
        return ref[:, start : start + size, :].reshape(-1, ref.shape[2])
    return ref[...]


def message_kernel(packed, peers, cap, cap_self, own_ref, oth_ref, pack_ref, out_ref):
    slots = pack_ref.shape[0]
    half = own_ref.shape[-1]
    at_count, at_pre, at_weight, at_sent, _ = pack_places(slots, half)
    own = part_of(own_ref, packed, cap, cap_self)
    oth = part_of(oth_ref, packed, cap, cap_self)
    weight = slice(at_weight, at_sent)
    both = dot(own, pack_ref[:half, weight]) + dot(oth, pack_ref[half : 2 * half, weight])
    count = pack_ref[:, at_count:at_pre].astype(F32)
    count = jnp.concatenate([count] * (half // 128), axis=1)
    pre = pack_ref[:, at_pre : at_pre + half].astype(F32)
    pre = pre + pack_ref[:, at_pre + half : at_weight].astype(F32)
    total = dot(pack_ref[:, :at_count], both[:, :half].astype(BF)) + count * both[:, half:] + pre
    out = total.astype(BF)
    if not packed:
        out_ref[...] = out
        return
    tiles = half // 128
    for tile in range(tiles):
        out_ref[:, tile * cap_self : (tile + 1) * cap_self, :] = out[
            :, tile * 128 : (tile + 1) * 128
        ].reshape(peers, cap_self, 128)
    sent = pack_ref[:peers, at_sent:].astype(F32)
    out_ref[:, tiles * cap_self :, :] = jnp.broadcast_to(sent[:, None, :], (peers, 16, 128)).astype(
        BF
    )


def attention_kernel(
    packed,
    cap,
    cap_self,
    *refs,
):
    own_refs, oth_refs, refs = (refs[:1], refs[1:2], refs[2:]) if packed else (
        refs[:2], refs[2:4], refs[4:]
    )
    wkvt_ref, nslot_ref, te_ref, wqt_ref, slot_t_ref, phase_ref, wout_ref, wself_ref = refs[:8]
    emb_ref, kv_w, value_ref = refs[8:]
    nown_ref, sown_ref = own_refs[0], own_refs[-1]
    noth_ref, soth_ref = oth_refs[0], oth_refs[-1]
    core = lax.axis_index("mp")
    half = wout_ref.shape[0]
    width = 2 * half
    size = width // HEADS
    heads = HEADS // 2
    mine, theirs = half_of(core, half), half_of(1 - core, half)
    fown = part_of(nown_ref, packed, 0, cap)
    foth = part_of(noth_ref, packed, 0, cap)
    slots = fown.shape[0]
    kv_w[:, :slots] = (dot_nt(wkvt_ref[:, mine], fown) + dot_nt(wkvt_ref[:, theirs], foth)).astype(BF)
    kv_w[:, slots:] = wkvt_ref[:, width:]
    xown = part_of(sown_ref, packed, cap, cap_self)
    xoth = part_of(soth_ref, packed, cap, cap_self)
    slots_s = xown.shape[0]
    te_self = encode_turns(phase_ref[...]).astype(BF)
    te_self = jnp.broadcast_to(te_self, (128, te_self.shape[1]))
    query = dot_nt(wqt_ref[:, mine], xown) + dot_nt(wqt_ref[:, theirs], xoth)
    query_te = dot_nt(wqt_ref[:, width:], te_self)
    query = (query + jnp.concatenate([query_te] * (slots_s // 128), axis=1)).astype(BF)
    find = jnp.concatenate(tall_one_hot(slot_t_ref, slots_s), axis=1)
    q = dot(query, find) * (1.0 / size**0.5)
    neigh, _, ends = te_ref.shape
    at = iota((slots, ends), 0)
    weights = []
    for k in range(neigh):
        line = jnp.concatenate([nslot_ref[j, k : k + 1, :] for j in range(2)], axis=1)
        right = jnp.concatenate([one_hot(at == line), te_ref[k]], axis=0)
        kv = dot(kv_w[...], right)
        value_ref[k] = kv[half:].astype(BF)
        score = q * kv[:half].astype(BF).astype(F32)
        score = [
            jnp.sum(score[h * size : (h + 1) * size], axis=0, keepdims=True) for h in range(heads)
        ]
        weights.append(jnp.exp(jnp.concatenate(score, axis=0)))
    total = weights[0]
    for k in range(1, neigh):
        total = total + weights[k]
    weights = [(w / total).astype(BF).astype(F32) for w in weights]
    att = []
    for h in range(heads):
        part = jnp.zeros((size, ends), F32)
        for k in range(neigh):
            value = value_ref[k, h * size : (h + 1) * size, :].astype(F32)
            part = part + weights[k][h : h + 1] * value
        att.append(part)
    att = jnp.concatenate(att, axis=0).T.astype(BF)
    events = ends // 2
    at = iota((events, slots_s), 1)
    find = [
        one_hot(at == down(slot_t_ref[j : j + 1, :].astype(F32), slots_s).astype(I32))
        for j in range(2)
    ]
    self_own = dot(jnp.concatenate(find, axis=0), xown).astype(BF)
    emb_ref[...] = (dot(att, wout_ref[...]) + dot(self_own, wself_ref[...])).astype(BF)


def sum_kernel(own_ref, oth_ref, out_ref):
    total = own_ref[...].astype(F32) + oth_ref[...].astype(F32)
    events = out_ref.shape[0]
    out_ref[...] = jnp.stack([total[:events], total[events:]], axis=1).astype(BF)


def update_kernel(
    packed,
    cap_self,
    own_ref,
    oth_ref,
    count_ref,
    serve_ref,
    win_ref,
    gh_ref,
    old_ref,
    base_ref,
    out_ref,
    put,
):
    core = lax.axis_index("mp")
    rows, half = base_ref.shape
    serve = serve_ref[0]
    slots = serve.size
    tiles = half // 128

    def messages(ref):
        if not packed:
            return ref[...]
        return jnp.concatenate(
            [
                ref[:, tile * cap_self : (tile + 1) * cap_self, :].reshape(slots, 128)
                for tile in range(tiles)
            ],
            axis=1,
        )

    line = row(serve)
    match = column(serve, 0, slots) == line
    same = one_hot(match)
    earlier = match & (iota((slots, slots), 0) < iota((slots, slots), 1))
    again = jnp.sum(jnp.where(earlier, 1.0, 0.0), axis=0, keepdims=True)
    line = jnp.where(again > 0, -1.0, line)
    step = rows // out_ref.parts
    for part in range(out_ref.parts):
        at = (iota((step, slots), 0) + part * step).astype(F32)
        put[part * step : (part + 1) * step, :] = one_hot(at == line)
    peers = slots // cap_self
    counts = count_ref[:, tiles * cap_self :, :][:, 0, :] if packed else count_ref[...]
    spread = dot(one_hot(iota((slots, peers), 0) // cap_self == iota((slots, peers), 1)), counts)
    lane = iota((slots, 128), 1)
    spread = jnp.where(iota((slots, 128), 0) % cap_self == lane, spread, 0.0).astype(BF)
    count = jnp.sum(dot(same, spread), axis=1, keepdims=True)
    inverse = 1.0 / jnp.maximum(count, 1.0)
    own = (dot(same, messages(own_ref)) * inverse).astype(BF)
    oth = (dot(same, messages(oth_ref)) * inverse).astype(BF)
    mine, theirs = half_of(core, half), half_of(1 - core, half)
    gi = [dot(own, win_ref[g, mine, :]) + dot(oth, win_ref[g, theirs, :]) for g in range(3)]
    reset = jax.nn.sigmoid(gi[0] + gh_ref[0])
    gate = jax.nn.sigmoid(gi[1] + gh_ref[1])
    cand = jnp.tanh(gi[2] + reset * gh_ref[2])
    old = old_ref[...].reshape(slots, half).astype(F32)
    fresh = jnp.where(count > 0, (1.0 - gate) * cand + gate * old, old).astype(BF)
    for part in range(out_ref.parts):
        at = slice(part * step, (part + 1) * step)
        moved = dot(put[at, :], fresh)
        out_ref[at, :] = (base_ref[at, :].astype(F32) + moved).astype(BF)
        out_ref.send(part)


def per_device(
    memory,
    ev_time,
    nbr_time,
    edge_feat,
    self_slot,
    nbr_slot,
    serve_self,
    serve_rows,
    freq,
    phase,
    w_query,
    w_key,
    w_value,
    w_out,
    w_self,
    w_msg_self,
    w_msg_other,
    w_msg_time,
    w_msg_edge,
    w_in,
    w_hid,
):
    owned, width = memory.shape
    half = w_out.shape[0]
    peers, cap = serve_rows.shape[1:]
    cap_self = serve_self.shape[2]
    events, _, neigh = nbr_slot.shape
    ends = 2 * events
    tdim = freq.shape[0]
    slots_n, slots_s = peers * cap, peers * cap_self
    packed = cap % 16 == 0 and cap_self % 16 == 0
    shape = jax.ShapeDtypeStruct

    core = lax.axis_index("mp")

    def call(kernel, out_shape, args, flops=0, scratch=(), limit=62, direct=(), views={}, parts=(), small=False):
        single = not isinstance(out_shape, (list, tuple))
        outs = [out_shape] if single else list(out_shape)
        parts = [*parts, *[1] * (len(outs) - len(parts))]
        size = sum(a.size * a.dtype.itemsize for a in (*args, *outs))
        whole, rooms = [], []
        for n, arg in enumerate(args):
            if n in direct:
                whole.append(None)
                continue
            view, room = views.get(n, (lambda ref: ref, arg.shape))
            whole.append(view)
            rooms.append(pltpu.VMEM(room, arg.dtype))
        rooms += [pltpu.VMEM(o.shape, o.dtype) for o in outs]
        return pl.pallas_call(
            functools.partial(staged, kernel, whole, parts),
            out_shape=out_shape,
            in_specs=[HBM if view else VMEM for view in whole],
            out_specs=HBM if single else [HBM] * len(outs),
            scratch_shapes=[
                *rooms,
                *scratch,
                pltpu.SemaphoreType.DMA((len(args),)),
                pltpu.SemaphoreType.DMA((len(outs), max(parts))),
            ],
            compiler_params=pltpu.CompilerParams(vmem_limit_bytes=limit * 1024 * 1024),
            cost_estimate=pl.CostEstimate(
                flops=int(flops), bytes_accessed=1 if small else int(size), transcendentals=0
            ),
        )(*args)

    def columns(rows):
        return (lambda ref: ref.at[:, half_of(lax.axis_index("mp"), half)], (rows, half))

    def stripe(part, size):
        return (
            lambda ref: ref.at[pl.ds(part * size, size), half_of(lax.axis_index("mp"), half)],
            (size, half),
        )

    def swap(x):
        return lax.ppermute(x, "mp", [(0, 1), (1, 0)])

    def exchange(x):
        return lax.all_to_all(x, "nodes", split_axis=0, concat_axis=0, tiled=True)

    flops_serve = 2 * (slots_n + slots_s) * owned * half
    if packed:
        served_shape = shape((peers, cap + cap_self, half), BF)
    else:
        served_shape = [shape((slots_n, half), BF), shape((slots_s, half), BF)]
    quarter = owned // 4
    served = call(
        functools.partial(serve_kernel, packed),
        served_shape,
        (serve_rows, serve_self, *[memory] * 4),
        flops_serve,
        [pltpu.VMEM((512, owned), BF)],
        views={2 + n: stripe(n, quarter) for n in range(4)},
        parts=[slots_s // 256] if packed and cap == cap_self else (),
    )
    if packed:
        old = served
        old_view = (lambda ref: ref.at[:, pl.ds(cap, cap_self), :], (peers, cap_self, half))
    else:
        served_n, old = served
        old_view = (lambda ref: ref, old.shape)
        served = jnp.concatenate(
            [served_n.reshape(peers, cap, half), old.reshape(peers, cap_self, half)], axis=1
        )
    fetched = exchange(served)

    away = lax.dynamic_slice_in_dim(
        jnp.concatenate([w_msg_self, w_msg_other, w_msg_time, w_msg_edge], axis=0),
        (1 - core) * half,
        half,
        1,
    )
    w_swap = swap(away)
    edge_t = edge_feat.T
    edge_swap = swap(edge_t)
    nslot = nbr_slot.transpose(1, 2, 0)
    slot_t = self_slot.T
    gh, te, wq_t, wkv_t = call(
        prepare_kernel,
        [
            shape((3, slots_s, half), F32),
            shape((neigh, tdim, ends), BF),
            shape((half, width + tdim), BF),
            shape((2 * half, width + tdim), BF),
        ],
        (
            serve_self,
            ev_time[None],
            nbr_time.transpose(1, 2, 0),
            freq[None],
            phase[None],
            memory,
            w_hid.transpose(1, 0, 2),
            w_query,
            w_key,
            w_value,
        ),
        2 * slots_s * (owned * width + width * 3 * half),
    )
    tpart = w_msg_time.shape[0]
    pack = call(
        functools.partial(slot_kernel, peers),
        shape((slots_s, pack_places(slots_s, half)[-1]), BF),
        (
            slot_t,
            te,
            edge_t,
            edge_swap,
            w_msg_time,
            w_msg_edge,
            w_msg_self,
            w_msg_other,
            w_swap,
        ),
        4 * slots_s * events * (slots_s + half),
        views={
            1: (lambda ref: ref.at[pl.ds(0, 1)], (1, tdim, ends)),
            4: columns(tpart),
            5: columns(w_msg_edge.shape[0]),
            6: columns(half),
            7: columns(half),
        },
    )
    base = call(
        place_kernel,
        shape((owned, half), BF),
        (serve_self, memory),
        0,
        views={1: columns(owned)},
        parts=[8],
    )

    fetched, te, pack, gh, base = lax.optimization_barrier((fetched, te, pack, gh, base))
    fetched_x = swap(fetched)
    if packed:
        both = (fetched, fetched_x)
        mine = (fetched, fetched_x)
        back_shape = shape((peers, (half // 128) * cap_self + 16, 128), BF)
    else:
        nbr = [f[:, :cap].reshape(slots_n, half) for f in (fetched, fetched_x)]
        mine = [f[:, cap:].reshape(slots_s, half) for f in (fetched, fetched_x)]
        both = (nbr[0], mine[0], nbr[1], mine[1])
        back_shape = shape((slots_s, half), BF)
    message = call(
        functools.partial(message_kernel, packed, peers, cap, cap_self),
        back_shape,
        (*mine, pack),
        2 * slots_s * half * (2 * width + slots_s),
        direct=(0, 1, 2),
        limit=50,
    )
    message, slot_t2 = lax.optimization_barrier((message, slot_t))
    part = call(
        functools.partial(attention_kernel, packed, cap, cap_self),
        shape((ends, width), BF),
        (*both, wkv_t, nslot, te, wq_t, slot_t2, phase[None], w_out, w_self),
        2 * ends * neigh * (slots_n + tdim) * width,
        [pltpu.VMEM((2 * half, slots_n + tdim), BF), pltpu.VMEM((neigh, half, ends), BF)],
        direct=range(len(both)),
        limit=52,
    )
    embedding = call(
        sum_kernel, shape((events, 2, width), BF), (part, swap(part)), direct=(0, 1), small=True
    )
    if not packed:
        message = jnp.concatenate(
            [
                message.reshape(peers, cap_self, half),
                jnp.pad(pack[:peers, -128:], ((0, 0), (0, half - 128)))[:, None],
            ],
            axis=1,
        )
    back = exchange(message)
    back, embedding = lax.optimization_barrier((back, embedding))
    back_x = swap(back)
    counts = back
    if not packed:
        back_x = back_x[:, :cap_self].reshape(slots_s, half)
        counts = back[:, cap_self, :128]
        back = back[:, :cap_self].reshape(slots_s, half)
    memory_out = call(
        functools.partial(update_kernel, packed, cap_self),
        shape((owned, half), BF),
        (back, back_x, counts, serve_self, w_in.transpose(1, 0, 2), gh, old, base),
        2 * slots_s * (slots_s * width + width * 3 * half + owned * half),
        [pltpu.VMEM((owned, slots_s), BF)],
        direct=(0, 1, 2),
        views={6: old_view},
        parts=[8],
        limit=50,
    )
    return (embedding, memory_out)


def solution(mesh):
    return jax.shard_map(
        per_device,
        mesh=mesh,
        in_specs=(
            P("nodes", None),
            P("nodes"),
            P("nodes", None, None),
            P("nodes", "mp"),
            P("nodes", None),
            P("nodes", None, None),
            P("nodes", None, None),
            P("nodes", None, None),
            P(),
            P(),
            P(None, "mp"),
            P(None, "mp"),
            P(None, "mp"),
            P("mp", None),
            P("mp", None),
            P("mp", None),
            P("mp", None),
            P("mp", None),
            P("mp", None),
            P(None, None, "mp"),
            P(None, None, "mp"),
        ),
        out_specs=(P("nodes", None, None), P("nodes", "mp")),
        check_vma=False,
    )
```

```python
import functools

import jax
import jax.numpy as jnp
from jax import lax
from jax.experimental import pallas as pl
from jax.experimental.pallas import tpu as pltpu
from jax.sharding import PartitionSpec as P

HEADS = 8
BF = jnp.bfloat16
F32 = jnp.float32
I32 = jnp.int32
VMEM = pl.BlockSpec(memory_space=pltpu.VMEM)
HBM = pl.BlockSpec(memory_space=pltpu.HBM)
TURN = 6.283185307179586
COS = (
    6.52861337,
    -25.9675685,
    60.1676231,
    -85.4501386,
    64.9391174,
    -19.7392045,
    0.999999989,
)


def dot(a, b):
    return jnp.dot(a, b, preferred_element_type=F32)


def dot_nt(a, b):
    return lax.dot_general(a, b, (((1,), (1,)), ((), ())), preferred_element_type=F32)


def iota(shape, dim):
    return lax.broadcasted_iota(I32, shape, dim)


class Operand:
    def __init__(self, copy, ref):
        self.copy, self.ref, self.shape = copy, ref, ref.shape
        copy.start()

    def wait(self):
        if self.copy is not None:
            self.copy.wait()
            self.copy = None

    def __getitem__(self, at):
        self.wait()
        return self.ref[at]


class Result:
    def __init__(self, room, ref, sems, parts):
        self.room, self.ref, self.sems, self.parts = room, ref, sems, parts
        self.shape, self.sent = room.shape, []

    def __setitem__(self, at, value):
        self.room[at] = value

    def __getitem__(self, at):
        return self.room[at]

    def send(self, part):
        size = self.shape[0] // self.parts
        at = pl.ds(part * size, size)
        copy = pltpu.make_async_copy(self.room.at[at], self.ref.at[at], self.sems.at[part])
        copy.start()
        self.sent.append((part, copy))

    def finish(self):
        done = [part for part, _ in self.sent]
        for part in range(self.parts):
            if part not in done:
                self.send(part)
        for _, copy in self.sent:
            copy.wait()


def staged(kernel, views, parts, *refs):
    count, outs = len(views), len(parts)
    ins, results, rest = refs[:count], refs[count : count + outs], list(refs[count + outs :])
    in_sems, out_sems = rest[-2:]
    rest = rest[:-2]
    operands = []
    for n, (ref, view) in enumerate(zip(ins, views)):
        if view is None:
            operands.append(ref)
        else:
            room = rest.pop(0)
            operands.append(Operand(pltpu.make_async_copy(view(ref), room, in_sems.at[n]), room))
    held = [
        Result(rest.pop(0), ref, out_sems.at[n], part)
        for n, (ref, part) in enumerate(zip(results, parts))
    ]
    kernel(*operands, *held, *rest)
    for operand in operands:
        if isinstance(operand, Operand):
            operand.wait()
    for result in held:
        result.finish()


def one_hot(mask):
    return jnp.where(mask, 1.0, 0.0).astype(BF)


def split(serve):
    high = lax.shift_right_logical(serve, 8)
    low = jnp.bitwise_and(serve, 255)
    return high.astype(F32).astype(BF), low.astype(F32).astype(BF)


def column(serve, start, count):
    peers, cap = serve.shape
    high, low = split(serve)
    pick = one_hot((iota((count, peers), 0) + start) // cap == iota((count, peers), 1))
    every = 256.0 * dot(pick, high) + dot(pick, low)
    mine = (iota((count, cap), 0) + start) % cap == iota((count, cap), 1)
    return jnp.sum(jnp.where(mine, every, 0.0), axis=1, keepdims=True)


def row(serve):
    peers, cap = serve.shape
    slots = peers * cap
    high, low = split(serve)
    pick = one_hot(iota((cap, slots), 1) % cap == iota((cap, slots), 0))
    every = 256.0 * dot(high, pick) + dot(low, pick)
    mine = iota((peers, slots), 1) // cap == iota((peers, slots), 0)
    return jnp.sum(jnp.where(mine, every, 0.0), axis=0, keepdims=True)


def rows_at(col, count):
    at = iota((col.shape[0], count), 1).astype(F32)
    return one_hot(at == col)


def half_of(core, half):
    return pl.ds(pl.multiple_of(core * half, half), half)


def serve_kernel(packed, rows_ref, self_ref, *refs):
    mems, outs, hot = refs[:4], refs[4:-1], refs[-1]
    depth, half = mems[0].shape
    count = len(mems) * depth
    step = 256
    rows, own = rows_ref[0], self_ref[0]
    jobs = []
    for table, serve in enumerate((rows, own)):
        jobs += [(start, table, serve) for start in range(0, serve.size, step)]
    jobs.sort(key=lambda job: (job[0], job[1]))
    early = hot.shape[0] // step
    for n, (start, table, serve) in enumerate(jobs[:early]):
        hot[n * step : (n + 1) * step, :] = rows_at(column(serve, start, step), count)
    for n, (start, table, serve) in enumerate(jobs):
        if n < early:
            at = hot[n * step : (n + 1) * step, :]
        else:
            at = rows_at(column(serve, start, step), count)
        picked = dot(at[:, :depth], mems[0][...])
        for part in range(1, len(mems)):
            picked = picked + dot(at[:, part * depth : (part + 1) * depth], mems[part][...])
        picked = picked.astype(BF)
        if packed:
            cap = serve.shape[1]
            first = table * rows.shape[1]
            outs[0][start // cap : (start + step) // cap, first : first + cap, :] = picked.reshape(
                step // cap, cap, half
            )
            if outs[0].parts > 1 and table == 1:
                outs[0].send(start // step)
        else:
            outs[table][start : start + step, :] = picked


def encode_turns(x):
    turns = x * (1.0 / TURN)
    u = turns - jnp.round(turns)
    square = u * u
    total = jnp.full_like(square, COS[0])
    for factor in COS[1:]:
        total = total * square + factor
    return total


def down(line, count):
    return jnp.broadcast_to(line, (count, line.shape[1])).T


def time_kernel(ev_ref, nbr_ref, freq_ref, phase_ref, wq_ref, wk_ref, wv_ref, te_ref, wqt_ref, wkvt_ref):
    neigh, tdim, ends = te_ref.shape
    events = ends // 2
    freq = down(freq_ref[...], events)
    phase = down(phase_ref[...], events)
    time = ev_ref[...]
    for k in range(neigh):
        for j in range(2):
            delta = (time - nbr_ref[j, k : k + 1, :]).astype(F32)
            enc = encode_turns(delta * freq + phase)
            te_ref[k, :, j * events : (j + 1) * events] = enc.astype(BF)
    half = wq_ref.shape[1]
    wqt_ref[...] = wq_ref[...].T
    wkvt_ref[:half, :] = wk_ref[...].T
    wkvt_ref[half:, :] = wv_ref[...].T


def tall_one_hot(slot_t_ref, slots):
    events = slot_t_ref.shape[1]
    at = iota((slots, events), 0)
    return [one_hot(at == slot_t_ref[j : j + 1, :]) for j in range(2)]


def pack_places(slots, half):
    at_pre = slots + 128
    at_weight = at_pre + 2 * half
    at_sent = at_weight + 2 * half
    return slots, at_pre, at_weight, at_sent, at_sent + 128


def slot_kernel(
    peers,
    slot_t_ref,
    te_ref,
    edge_ref,
    edge_x_ref,
    wt_ref,
    we_ref,
    ws_ref,
    wo_ref,
    wx_ref,
    pack_ref,
):
    core = lax.axis_index("mp")
    slots = pack_ref.shape[0]
    part, half = wt_ref.shape
    tall = tall_one_hot(slot_t_ref, slots)
    events = tall[0].shape[1]
    both = tall[0] + tall[1]
    at_count, at_pre, at_weight, at_sent = pack_places(slots, half)[:4]
    pack_ref[:, :at_count] = (dot_nt(tall[0], tall[1]) + dot_nt(tall[1], tall[0])).astype(BF)
    count = dot_nt(both, jnp.ones((128, events), BF))
    pack_ref[:, at_count:at_pre] = count.astype(BF)
    cap = slots // peers
    place = iota((slots, 128), 0) % cap == iota((slots, 128), 1)
    owner = one_hot(iota((peers, slots), 1) // cap == iota((peers, slots), 0))
    pack_ref[:peers, at_sent:] = dot(owner, jnp.where(place, count, 0.0).astype(BF)).astype(BF)
    pack_ref[peers:, at_sent:] = jnp.zeros((slots - peers, 128), BF)
    pack_ref[:half, at_weight : at_weight + half] = wo_ref[...]
    pack_ref[:half, at_weight + half : at_sent] = ws_ref[...]
    pack_ref[half : 2 * half, at_weight : at_weight + half] = wx_ref[half : 2 * half, :]
    pack_ref[half : 2 * half, at_weight + half : at_sent] = wx_ref[:half, :]
    mine, theirs = wt_ref[...], wx_ref[2 * half : 2 * half + part, :]
    first = core == 0
    weight = jnp.concatenate(
        [
            jnp.where(first, mine, theirs),
            jnp.where(first, theirs, mine),
            we_ref[...],
            wx_ref[2 * half + part :, :],
        ],
        axis=0,
    )
    edge = jnp.concatenate([edge_ref[...], edge_x_ref[...]], axis=0)
    value = jnp.concatenate(
        [dot_nt(jnp.concatenate(tall, axis=1), te_ref[0]), dot_nt(both, edge)], axis=1
    )
    high = value.astype(BF)
    low = (value - high.astype(F32)).astype(BF)
    pre = dot(high, weight) + dot(low, weight)
    high = pre.astype(BF)
    pack_ref[:, at_pre : at_pre + half] = high
    pack_ref[:, at_pre + half : at_weight] = (pre - high.astype(F32)).astype(BF)


def prepare_kernel(
    self_ref,
    ev_ref,
    nbr_ref,
    freq_ref,
    phase_ref,
    mem_ref,
    whid_ref,
    wq_ref,
    wk_ref,
    wv_ref,
    gh_ref,
    te_ref,
    wqt_ref,
    wkvt_ref,
):
    time_kernel(ev_ref, nbr_ref, freq_ref, phase_ref, wq_ref, wk_ref, wv_ref, te_ref, wqt_ref, wkvt_ref)
    te_ref.send(0)
    wqt_ref.send(0)
    wkvt_ref.send(0)
    count, width = mem_ref.shape
    serve = self_ref[0]
    slots = serve.size
    col = column(serve, 0, slots)
    for start in range(0, slots, 256):
        at = slice(start, start + 256)
        picked = dot(rows_at(col[at], count), mem_ref[...]).astype(BF)
        for g in range(3):
            gh_ref[g, at, :] = dot(picked, whid_ref[g])


def place_kernel(self_ref, mem_ref, base_ref):
    count, half = mem_ref.shape
    serve = self_ref[0]
    line = row(serve)
    step = count // base_ref.parts
    for part in range(base_ref.parts):
        at = slice(part * step, (part + 1) * step)
        hit = (iota((step, serve.size), 0) + part * step).astype(F32) == line
        served = jnp.max(jnp.where(hit, 1.0, 0.0), axis=1, keepdims=True)
        base_ref[at, :] = (mem_ref[at, :].astype(F32) * (1.0 - served)).astype(BF)
        base_ref.send(part)


def part_of(ref, packed, start, size):
    if packed:
        return ref[:, start : start + size, :].reshape(-1, ref.shape[2])
    return ref[...]


def message_part(own, pack_ref, first, half):
    slots = pack_ref.shape[0]
    at_count, at_pre, at_weight, at_sent, _ = pack_places(slots, half)
    both = dot(own, pack_ref[first : first + half, at_weight:at_sent])
    count = pack_ref[:, at_count:at_pre].astype(F32)
    count = jnp.concatenate([count] * (half // 128), axis=1)
    return dot(pack_ref[:, :at_count], both[:, :half].astype(BF)) + count * both[:, half:]


def own_message_kernel(packed, cap, cap_self, own_ref, pack_ref, total_ref):
    half = own_ref.shape[-1]
    _, at_pre, at_weight, _, _ = pack_places(pack_ref.shape[0], half)
    pre = pack_ref[:, at_pre : at_pre + half].astype(F32)
    pre = pre + pack_ref[:, at_pre + half : at_weight].astype(F32)
    own = part_of(own_ref, packed, cap, cap_self)
    total_ref[...] = message_part(own, pack_ref, 0, half) + pre


def message_kernel(packed, peers, cap, cap_self, oth_ref, pack_ref, total_ref, out_ref):
    half = oth_ref.shape[-1]
    at_sent = pack_places(pack_ref.shape[0], half)[3]
    oth = part_of(oth_ref, packed, cap, cap_self)
    out = (total_ref[...] + message_part(oth, pack_ref, half, half)).astype(BF)
    if not packed:
        out_ref[...] = out
        return
    tiles = half // 128
    for tile in range(tiles):
        out_ref[:, tile * cap_self : (tile + 1) * cap_self, :] = out[
            :, tile * 128 : (tile + 1) * 128
        ].reshape(peers, cap_self, 128)
    sent = pack_ref[:peers, at_sent:].astype(F32)
    out_ref[:, tiles * cap_self :, :] = jnp.broadcast_to(sent[:, None, :], (peers, 16, 128)).astype(
        BF
    )


def attention_kernel(
    packed,
    cap,
    cap_self,
    *refs,
):
    own_refs, oth_refs, refs = (refs[:1], refs[1:2], refs[2:]) if packed else (
        refs[:2], refs[2:4], refs[4:]
    )
    wkvt_ref, nslot_ref, te_ref, wqt_ref, slot_t_ref, phase_ref, wout_ref, wself_ref = refs[:8]
    emb_ref, kv_w, value_ref = refs[8:]
    nown_ref, sown_ref = own_refs[0], own_refs[-1]
    noth_ref, soth_ref = oth_refs[0], oth_refs[-1]
    core = lax.axis_index("mp")
    half = wout_ref.shape[0]
    width = 2 * half
    size = width // HEADS
    heads = HEADS // 2
    mine, theirs = half_of(core, half), half_of(1 - core, half)
    fown = part_of(nown_ref, packed, 0, cap)
    foth = part_of(noth_ref, packed, 0, cap)
    slots = fown.shape[0]
    kv_w[:, :slots] = (dot_nt(wkvt_ref[:, mine], fown) + dot_nt(wkvt_ref[:, theirs], foth)).astype(BF)
    kv_w[:, slots:] = wkvt_ref[:, width:]
    xown = part_of(sown_ref, packed, cap, cap_self)
    xoth = part_of(soth_ref, packed, cap, cap_self)
    slots_s = xown.shape[0]
    te_self = encode_turns(phase_ref[...]).astype(BF)
    te_self = jnp.broadcast_to(te_self, (128, te_self.shape[1]))
    query = dot_nt(wqt_ref[:, mine], xown) + dot_nt(wqt_ref[:, theirs], xoth)
    query_te = dot_nt(wqt_ref[:, width:], te_self)
    query = (query + jnp.concatenate([query_te] * (slots_s // 128), axis=1)).astype(BF)
    find = jnp.concatenate(tall_one_hot(slot_t_ref, slots_s), axis=1)
    q = dot(query, find) * (1.0 / size**0.5)
    neigh, _, ends = te_ref.shape
    at = iota((slots, ends), 0)
    weights = []
    for k in range(neigh):
        line = jnp.concatenate([nslot_ref[j, k : k + 1, :] for j in range(2)], axis=1)
        right = jnp.concatenate([one_hot(at == line), te_ref[k]], axis=0)
        kv = dot(kv_w[...], right)
        value_ref[k] = kv[half:].astype(BF)
        score = q * kv[:half].astype(BF).astype(F32)
        score = [
            jnp.sum(score[h * size : (h + 1) * size], axis=0, keepdims=True) for h in range(heads)
        ]
        weights.append(jnp.exp(jnp.concatenate(score, axis=0)))
    total = weights[0]
    for k in range(1, neigh):
        total = total + weights[k]
    weights = [(w / total).astype(BF).astype(F32) for w in weights]
    att = []
    for h in range(heads):
        part = jnp.zeros((size, ends), F32)
        for k in range(neigh):
            value = value_ref[k, h * size : (h + 1) * size, :].astype(F32)
            part = part + weights[k][h : h + 1] * value
        att.append(part)
    att = jnp.concatenate(att, axis=0).T.astype(BF)
    events = ends // 2
    at = iota((events, slots_s), 1)
    find = [
        one_hot(at == down(slot_t_ref[j : j + 1, :].astype(F32), slots_s).astype(I32))
        for j in range(2)
    ]
    self_own = dot(jnp.concatenate(find, axis=0), xown).astype(BF)
    emb_ref[...] = (dot(att, wout_ref[...]) + dot(self_own, wself_ref[...])).astype(BF)


def sum_kernel(own_ref, oth_ref, out_ref):
    total = own_ref[...].astype(F32) + oth_ref[...].astype(F32)
    events = out_ref.shape[0]
    out_ref[...] = jnp.stack([total[:events], total[events:]], axis=1).astype(BF)


def update_kernel(
    packed,
    cap_self,
    own_ref,
    oth_ref,
    count_ref,
    serve_ref,
    win_ref,
    gh_ref,
    old_ref,
    base_ref,
    out_ref,
    put,
):
    core = lax.axis_index("mp")
    rows, half = base_ref.shape
    serve = serve_ref[0]
    slots = serve.size
    tiles = half // 128

    def messages(ref):
        if not packed:
            return ref[...]
        return jnp.concatenate(
            [
                ref[:, tile * cap_self : (tile + 1) * cap_self, :].reshape(slots, 128)
                for tile in range(tiles)
            ],
            axis=1,
        )

    line = row(serve)
    match = column(serve, 0, slots) == line
    same = one_hot(match)
    earlier = match & (iota((slots, slots), 0) < iota((slots, slots), 1))
    again = jnp.sum(jnp.where(earlier, 1.0, 0.0), axis=0, keepdims=True)
    line = jnp.where(again > 0, -1.0, line)
    step = rows // out_ref.parts
    for part in range(out_ref.parts):
        at = (iota((step, slots), 0) + part * step).astype(F32)
        put[part * step : (part + 1) * step, :] = one_hot(at == line)
    peers = slots // cap_self
    counts = count_ref[:, tiles * cap_self :, :][:, 0, :] if packed else count_ref[...]
    spread = dot(one_hot(iota((slots, peers), 0) // cap_self == iota((slots, peers), 1)), counts)
    lane = iota((slots, 128), 1)
    spread = jnp.where(iota((slots, 128), 0) % cap_self == lane, spread, 0.0).astype(BF)
    count = jnp.sum(dot(same, spread), axis=1, keepdims=True)
    inverse = 1.0 / jnp.maximum(count, 1.0)
    own = (dot(same, messages(own_ref)) * inverse).astype(BF)
    oth = (dot(same, messages(oth_ref)) * inverse).astype(BF)
    mine, theirs = half_of(core, half), half_of(1 - core, half)
    gi = [dot(own, win_ref[g, mine, :]) + dot(oth, win_ref[g, theirs, :]) for g in range(3)]
    reset = jax.nn.sigmoid(gi[0] + gh_ref[0])
    gate = jax.nn.sigmoid(gi[1] + gh_ref[1])
    cand = jnp.tanh(gi[2] + reset * gh_ref[2])
    old = old_ref[...].reshape(slots, half).astype(F32)
    fresh = jnp.where(count > 0, (1.0 - gate) * cand + gate * old, old).astype(BF)
    for part in range(out_ref.parts):
        at = slice(part * step, (part + 1) * step)
        moved = dot(put[at, :], fresh)
        out_ref[at, :] = (base_ref[at, :].astype(F32) + moved).astype(BF)
        out_ref.send(part)


def per_device(
    memory,
    ev_time,
    nbr_time,
    edge_feat,
    self_slot,
    nbr_slot,
    serve_self,
    serve_rows,
    freq,
    phase,
    w_query,
    w_key,
    w_value,
    w_out,
    w_self,
    w_msg_self,
    w_msg_other,
    w_msg_time,
    w_msg_edge,
    w_in,
    w_hid,
):
    owned, width = memory.shape
    half = w_out.shape[0]
    peers, cap = serve_rows.shape[1:]
    cap_self = serve_self.shape[2]
    events, _, neigh = nbr_slot.shape
    ends = 2 * events
    tdim = freq.shape[0]
    slots_n, slots_s = peers * cap, peers * cap_self
    packed = cap % 16 == 0 and cap_self % 16 == 0
    shape = jax.ShapeDtypeStruct

    core = lax.axis_index("mp")

    def call(kernel, out_shape, args, flops=0, scratch=(), limit=62, direct=(), views={}, parts=(), small=False):
        single = not isinstance(out_shape, (list, tuple))
        outs = [out_shape] if single else list(out_shape)
        parts = [*parts, *[1] * (len(outs) - len(parts))]
        size = sum(a.size * a.dtype.itemsize for a in (*args, *outs))
        whole, rooms = [], []
        for n, arg in enumerate(args):
            if n in direct:
                whole.append(None)
                continue
            view, room = views.get(n, (lambda ref: ref, arg.shape))
            whole.append(view)
            rooms.append(pltpu.VMEM(room, arg.dtype))
        rooms += [pltpu.VMEM(o.shape, o.dtype) for o in outs]
        return pl.pallas_call(
            functools.partial(staged, kernel, whole, parts),
            out_shape=out_shape,
            in_specs=[HBM if view else VMEM for view in whole],
            out_specs=HBM if single else [HBM] * len(outs),
            scratch_shapes=[
                *rooms,
                *scratch,
                pltpu.SemaphoreType.DMA((len(args),)),
                pltpu.SemaphoreType.DMA((len(outs), max(parts))),
            ],
            compiler_params=pltpu.CompilerParams(vmem_limit_bytes=limit * 1024 * 1024),
            cost_estimate=pl.CostEstimate(
                flops=int(flops), bytes_accessed=1 if small else int(size), transcendentals=0
            ),
        )(*args)

    def plain(kernel, out_shape, args, flops, limit):
        size = sum(a.size * a.dtype.itemsize for a in (*args, out_shape))
        return pl.pallas_call(
            kernel,
            out_shape=out_shape,
            in_specs=[VMEM] * len(args),
            out_specs=VMEM,
            compiler_params=pltpu.CompilerParams(vmem_limit_bytes=limit * 1024 * 1024),
            cost_estimate=pl.CostEstimate(
                flops=int(flops), bytes_accessed=int(size), transcendentals=0
            ),
        )(*args)

    def columns(rows):
        return (lambda ref: ref.at[:, half_of(lax.axis_index("mp"), half)], (rows, half))

    def stripe(part, size):
        return (
            lambda ref: ref.at[pl.ds(part * size, size), half_of(lax.axis_index("mp"), half)],
            (size, half),
        )

    def swap(x):
        return lax.ppermute(x, "mp", [(0, 1), (1, 0)])

    def exchange(x):
        return lax.all_to_all(x, "nodes", split_axis=0, concat_axis=0, tiled=True)

    flops_serve = 2 * (slots_n + slots_s) * owned * half
    if packed:
        served_shape = shape((peers, cap + cap_self, half), BF)
    else:
        served_shape = [shape((slots_n, half), BF), shape((slots_s, half), BF)]
    quarter = owned // 4
    served = call(
        functools.partial(serve_kernel, packed),
        served_shape,
        (serve_rows, serve_self, *[memory] * 4),
        flops_serve,
        [pltpu.VMEM((512, owned), BF)],
        views={2 + n: stripe(n, quarter) for n in range(4)},
        parts=[slots_s // 256] if packed and cap == cap_self else (),
    )
    if packed:
        old = served
        old_view = (lambda ref: ref.at[:, pl.ds(cap, cap_self), :], (peers, cap_self, half))
    else:
        served_n, old = served
        old_view = (lambda ref: ref, old.shape)
        served = jnp.concatenate(
            [served_n.reshape(peers, cap, half), old.reshape(peers, cap_self, half)], axis=1
        )
    fetched = exchange(served)

    away = lax.dynamic_slice_in_dim(
        jnp.concatenate([w_msg_self, w_msg_other, w_msg_time, w_msg_edge], axis=0),
        (1 - core) * half,
        half,
        1,
    )
    w_swap = swap(away)
    edge_t = edge_feat.T
    edge_swap = swap(edge_t)
    nslot = nbr_slot.transpose(1, 2, 0)
    slot_t = self_slot.T
    gh, te, wq_t, wkv_t = call(
        prepare_kernel,
        [
            shape((3, slots_s, half), F32),
            shape((neigh, tdim, ends), BF),
            shape((half, width + tdim), BF),
            shape((2 * half, width + tdim), BF),
        ],
        (
            serve_self,
            ev_time[None],
            nbr_time.transpose(1, 2, 0),
            freq[None],
            phase[None],
            memory,
            w_hid.transpose(1, 0, 2),
            w_query,
            w_key,
            w_value,
        ),
        2 * slots_s * (owned * width + width * 3 * half),
    )
    tpart = w_msg_time.shape[0]
    pack = call(
        functools.partial(slot_kernel, peers),
        shape((slots_s, pack_places(slots_s, half)[-1]), BF),
        (
            slot_t,
            te,
            edge_t,
            edge_swap,
            w_msg_time,
            w_msg_edge,
            w_msg_self,
            w_msg_other,
            w_swap,
        ),
        4 * slots_s * events * (slots_s + half),
        views={
            1: (lambda ref: ref.at[pl.ds(0, 1)], (1, tdim, ends)),
            4: columns(tpart),
            5: columns(w_msg_edge.shape[0]),
            6: columns(half),
            7: columns(half),
        },
    )
    base = call(
        place_kernel,
        shape((owned, half), BF),
        (serve_self, memory),
        0,
        views={1: columns(owned)},
        parts=[8],
    )

    fetched, te, pack, gh, base = lax.optimization_barrier((fetched, te, pack, gh, base))
    fetched_x = swap(fetched)
    if packed:
        both = (fetched, fetched_x)
        mine = (fetched, fetched_x)
        back_shape = shape((peers, (half // 128) * cap_self + 16, 128), BF)
    else:
        nbr = [f[:, :cap].reshape(slots_n, half) for f in (fetched, fetched_x)]
        mine = [f[:, cap:].reshape(slots_s, half) for f in (fetched, fetched_x)]
        both = (nbr[0], mine[0], nbr[1], mine[1])
        back_shape = shape((slots_s, half), BF)
    total = plain(
        functools.partial(own_message_kernel, packed, cap, cap_self),
        shape((slots_s, half), F32),
        (mine[0], pack),
        slots_s * half * (2 * width + slots_s),
        50,
    )
    message = plain(
        functools.partial(message_kernel, packed, peers, cap, cap_self),
        back_shape,
        (mine[1], pack, total),
        slots_s * half * (2 * width + slots_s),
        50,
    )
    message, slot_t2 = lax.optimization_barrier((message, slot_t))
    part = call(
        functools.partial(attention_kernel, packed, cap, cap_self),
        shape((ends, width), BF),
        (*both, wkv_t, nslot, te, wq_t, slot_t2, phase[None], w_out, w_self),
        2 * ends * neigh * (slots_n + tdim) * width,
        [pltpu.VMEM((2 * half, slots_n + tdim), BF), pltpu.VMEM((neigh, half, ends), BF)],
        direct=range(len(both)),
        limit=62,
    )
    embedding = call(
        sum_kernel, shape((events, 2, width), BF), (part, swap(part)), direct=(0, 1), small=True, limit=52
    )
    if not packed:
        message = jnp.concatenate(
            [
                message.reshape(peers, cap_self, half),
                jnp.pad(pack[:peers, -128:], ((0, 0), (0, half - 128)))[:, None],
            ],
            axis=1,
        )
    back = exchange(message)
    back, embedding = lax.optimization_barrier((back, embedding))
    back_x = swap(back)
    counts = back
    if not packed:
        back_x = back_x[:, :cap_self].reshape(slots_s, half)
        counts = back[:, cap_self, :128]
        back = back[:, :cap_self].reshape(slots_s, half)
    memory_out = call(
        functools.partial(update_kernel, packed, cap_self),
        shape((owned, half), BF),
        (back, back_x, counts, serve_self, w_in.transpose(1, 0, 2), gh, old, base),
        2 * slots_s * (slots_s * width + width * 3 * half + owned * half),
        [pltpu.VMEM((owned, slots_s), BF)],
        direct=(0, 1, 2),
        views={6: old_view},
        parts=[8],
        limit=53,
    )
    return (embedding, memory_out)


def solution(mesh):
    return jax.shard_map(
        per_device,
        mesh=mesh,
        in_specs=(
            P("nodes", None),
            P("nodes"),
            P("nodes", None, None),
            P("nodes", "mp"),
            P("nodes", None),
            P("nodes", None, None),
            P("nodes", None, None),
            P("nodes", None, None),
            P(),
            P(),
            P(None, "mp"),
            P(None, "mp"),
            P(None, "mp"),
            P("mp", None),
            P("mp", None),
            P("mp", None),
            P("mp", None),
            P("mp", None),
            P("mp", None),
            P(None, None, "mp"),
            P(None, None, "mp"),
        ),
        out_specs=(P("nodes", None, None), P("nodes", "mp")),
        check_vma=False,
    )
```

```python
import functools

import jax
import jax.numpy as jnp
from jax import lax
from jax.experimental import pallas as pl
from jax.experimental.pallas import tpu as pltpu
from jax.sharding import PartitionSpec as P

HEADS = 8
BF = jnp.bfloat16
F32 = jnp.float32
I32 = jnp.int32
VMEM = pl.BlockSpec(memory_space=pltpu.VMEM)
HBM = pl.BlockSpec(memory_space=pltpu.HBM)
TURN = 6.283185307179586
COS = (
    6.52861337,
    -25.9675685,
    60.1676231,
    -85.4501386,
    64.9391174,
    -19.7392045,
    0.999999989,
)


def dot(a, b):
    return jnp.dot(a, b, preferred_element_type=F32)


def dot_nt(a, b):
    return lax.dot_general(a, b, (((1,), (1,)), ((), ())), preferred_element_type=F32)


def iota(shape, dim):
    return lax.broadcasted_iota(I32, shape, dim)


class Operand:
    def __init__(self, copy, ref):
        self.copy, self.ref, self.shape = copy, ref, ref.shape
        self.started = False

    def start(self):
        if not self.started:
            self.copy.start()
            self.started = True

    def wait(self):
        if self.copy is not None:
            self.start()
            self.copy.wait()
            self.copy = None

    def __getitem__(self, at):
        self.wait()
        return self.ref[at]


class Result:
    def __init__(self, room, ref, sems, parts):
        self.room, self.ref, self.sems, self.parts = room, ref, sems, parts
        self.shape, self.sent = room.shape, []

    def __setitem__(self, at, value):
        self.room[at] = value

    def __getitem__(self, at):
        return self.room[at]

    def send(self, part):
        size = self.shape[0] // self.parts
        at = pl.ds(part * size, size)
        copy = pltpu.make_async_copy(self.room.at[at], self.ref.at[at], self.sems.at[part])
        copy.start()
        self.sent.append((part, copy))

    def finish(self):
        done = [part for part, _ in self.sent]
        for part in range(self.parts):
            if part not in done:
                self.send(part)
        for _, copy in self.sent:
            copy.wait()


def staged(kernel, views, parts, late, *refs):
    count, outs = len(views), len(parts)
    ins, results, rest = refs[:count], refs[count : count + outs], list(refs[count + outs :])
    in_sems, out_sems = rest[-2:]
    rest = rest[:-2]
    operands = []
    for n, (ref, view) in enumerate(zip(ins, views)):
        if view is None:
            operands.append(ref)
        else:
            room = rest.pop(0)
            operands.append(Operand(pltpu.make_async_copy(view(ref), room, in_sems.at[n]), room))
    for n, operand in enumerate(operands):
        if isinstance(operand, Operand) and n not in late:
            operand.start()
    held = [
        Result(rest.pop(0), ref, out_sems.at[n], part)
        for n, (ref, part) in enumerate(zip(results, parts))
    ]
    kernel(*operands, *held, *rest)
    for operand in operands:
        if isinstance(operand, Operand):
            operand.wait()
    for result in held:
        result.finish()


def one_hot(mask):
    return jnp.where(mask, 1.0, 0.0).astype(BF)


def split(serve):
    high = lax.shift_right_logical(serve, 8)
    low = jnp.bitwise_and(serve, 255)
    return high.astype(F32).astype(BF), low.astype(F32).astype(BF)


def column(serve, start, count):
    peers, cap = serve.shape
    high, low = split(serve)
    pick = one_hot((iota((count, peers), 0) + start) // cap == iota((count, peers), 1))
    every = 256.0 * dot(pick, high) + dot(pick, low)
    mine = (iota((count, cap), 0) + start) % cap == iota((count, cap), 1)
    return jnp.sum(jnp.where(mine, every, 0.0), axis=1, keepdims=True)


def row(serve):
    peers, cap = serve.shape
    slots = peers * cap
    high, low = split(serve)
    pick = one_hot(iota((cap, slots), 1) % cap == iota((cap, slots), 0))
    every = 256.0 * dot(high, pick) + dot(low, pick)
    mine = iota((peers, slots), 1) // cap == iota((peers, slots), 0)
    return jnp.sum(jnp.where(mine, every, 0.0), axis=0, keepdims=True)


def hot_rows(line, start, count):
    width = line.shape[1]
    near = (line - start).astype(I32)
    near = jnp.where((near >= 0) & (near < count), near, -1)
    near = jnp.broadcast_to(near, (16, width)).astype(jnp.int16)
    near = jnp.concatenate([near] * (count // 16), axis=0)
    at = lax.broadcasted_iota(jnp.int16, (count, width), 0)
    return jnp.where(at == near, jnp.ones((), BF), jnp.zeros((), BF))


def rows_at(col, count):
    near = jnp.broadcast_to(col, (col.shape[0], 128)).astype(I32).astype(jnp.int16)
    near = jnp.concatenate([near] * (count // 128), axis=1)
    at = lax.broadcasted_iota(jnp.int16, near.shape, 1)
    return jnp.where(at == near, jnp.ones((), BF), jnp.zeros((), BF))


def half_of(core, half):
    return pl.ds(pl.multiple_of(core * half, half), half)


def serve_kernel(packed, rows_ref, self_ref, *refs):
    mems, outs, hot = refs[:1], refs[1:-1], refs[-1]
    depth, half = mems[0].shape
    count = len(mems) * depth
    step = 256
    rows, own = rows_ref[0], self_ref[0]
    jobs = []
    for table, serve in enumerate((rows, own)):
        jobs += [(start, table, serve) for start in range(0, serve.size, step)]
    jobs.sort(key=lambda job: (job[0], job[1]))
    early = hot.shape[0] // step
    for n, (start, table, serve) in enumerate(jobs[:early]):
        hot[n * step : (n + 1) * step, :] = rows_at(column(serve, start, step), count)
    for n, (start, table, serve) in enumerate(jobs):
        if n < early:
            at = hot[n * step : (n + 1) * step, :]
        else:
            at = rows_at(column(serve, start, step), count)
        picked = dot(at[:, :depth], mems[0][...])
        for part in range(1, len(mems)):
            picked = picked + dot(at[:, part * depth : (part + 1) * depth], mems[part][...])
        picked = picked.astype(BF)
        if packed:
            cap = serve.shape[1]
            first = table * rows.shape[1]
            outs[0][start // cap : (start + step) // cap, first : first + cap, :] = picked.reshape(
                step // cap, cap, half
            )
            if outs[0].parts > 1 and table == 1:
                outs[0].send(start // step)
        else:
            outs[table][start : start + step, :] = picked


def encode_turns(x):
    turns = x * (1.0 / TURN)
    u = turns - jnp.round(turns)
    square = u * u
    total = jnp.full_like(square, COS[0])
    for factor in COS[1:]:
        total = total * square + factor
    return total


def down(line, count):
    return jnp.broadcast_to(line, (count, line.shape[1])).T


def time_kernel(ev_ref, nbr_ref, freq_ref, phase_ref, wq_ref, wk_ref, wv_ref, te_ref, wqt_ref, wkvt_ref):
    neigh, tdim, ends = te_ref.shape
    events = ends // 2
    freq = down(freq_ref[...], events)
    phase = down(phase_ref[...], events)
    time = ev_ref[...]
    for k in range(neigh):
        for j in range(2):
            delta = (time - nbr_ref[j, k : k + 1, :]).astype(F32)
            enc = encode_turns(delta * freq + phase)
            te_ref[k, :, j * events : (j + 1) * events] = enc.astype(BF)
    half = wq_ref.shape[1]
    wqt_ref[...] = wq_ref[...].T
    wkvt_ref[:half, :] = wk_ref[...].T
    wkvt_ref[half:, :] = wv_ref[...].T


def tall_one_hot(slot_t_ref, slots):
    events = slot_t_ref.shape[1]
    at = iota((slots, events), 0)
    return [one_hot(at == slot_t_ref[j : j + 1, :]) for j in range(2)]


def pack_places(slots, half):
    at_pre = slots + 128
    at_weight = at_pre + 2 * half
    at_sent = at_weight + 2 * half
    return slots, at_pre, at_weight, at_sent, at_sent + 128


def slot_kernel(
    peers,
    slot_t_ref,
    te_ref,
    edge_ref,
    edge_x_ref,
    wt_ref,
    we_ref,
    ws_ref,
    wo_ref,
    wx_ref,
    pack_ref,
):
    core = lax.axis_index("mp")
    slots = pack_ref.shape[0]
    part, half = wt_ref.shape
    tall = tall_one_hot(slot_t_ref, slots)
    events = tall[0].shape[1]
    both = tall[0] + tall[1]
    at_count, at_pre, at_weight, at_sent = pack_places(slots, half)[:4]
    pack_ref[:, :at_count] = (dot_nt(tall[0], tall[1]) + dot_nt(tall[1], tall[0])).astype(BF)
    count = dot_nt(both, jnp.ones((128, events), BF))
    pack_ref[:, at_count:at_pre] = count.astype(BF)
    cap = slots // peers
    place = iota((slots, 128), 0) % cap == iota((slots, 128), 1)
    owner = one_hot(iota((peers, slots), 1) // cap == iota((peers, slots), 0))
    pack_ref[:peers, at_sent:] = dot(owner, jnp.where(place, count, 0.0).astype(BF)).astype(BF)
    pack_ref[peers:, at_sent:] = jnp.zeros((slots - peers, 128), BF)
    pack_ref[:half, at_weight : at_weight + half] = wo_ref[...]
    pack_ref[:half, at_weight + half : at_sent] = ws_ref[...]
    pack_ref[half : 2 * half, at_weight : at_weight + half] = wx_ref[half : 2 * half, :]
    pack_ref[half : 2 * half, at_weight + half : at_sent] = wx_ref[:half, :]
    mine, theirs = wt_ref[...], wx_ref[2 * half : 2 * half + part, :]
    first = core == 0
    weight = jnp.concatenate(
        [
            jnp.where(first, mine, theirs),
            jnp.where(first, theirs, mine),
            we_ref[...],
            wx_ref[2 * half + part :, :],
        ],
        axis=0,
    )
    edge = jnp.concatenate([edge_ref[...], edge_x_ref[...]], axis=0)
    value = jnp.concatenate(
        [dot_nt(jnp.concatenate(tall, axis=1), te_ref[0]), dot_nt(both, edge)], axis=1
    )
    high = value.astype(BF)
    low = (value - high.astype(F32)).astype(BF)
    pre = dot(high, weight) + dot(low, weight)
    high = pre.astype(BF)
    pack_ref[:, at_pre : at_pre + half] = high
    pack_ref[:, at_pre + half : at_weight] = (pre - high.astype(F32)).astype(BF)


def prepare_kernel(
    self_ref,
    ev_ref,
    nbr_ref,
    freq_ref,
    phase_ref,
    mem_ref,
    whid_ref,
    wq_ref,
    wk_ref,
    wv_ref,
    gh_ref,
    te_ref,
    wqt_ref,
    wkvt_ref,
    base_ref,
):
    time_kernel(ev_ref, nbr_ref, freq_ref, phase_ref, wq_ref, wk_ref, wv_ref, te_ref, wqt_ref, wkvt_ref)
    te_ref.send(0)
    wqt_ref.send(0)
    wkvt_ref.send(0)
    count, width = mem_ref.shape
    serve = self_ref[0]
    slots = serve.size
    col = column(serve, 0, slots)
    for start in range(0, slots, 256):
        at = slice(start, start + 256)
        picked = dot(rows_at(col[at], count), mem_ref[...]).astype(BF)
        for g in range(3):
            gh_ref[g, at, :] = dot(picked, whid_ref[g])
    gh_ref.send(0)
    line = row(serve)
    cols = half_of(lax.axis_index("mp"), width // 2)
    step = count // base_ref.parts
    for part in range(base_ref.parts):
        at = slice(part * step, (part + 1) * step)
        hit = hot_rows(line, part * step, step)
        served = dot(hit, jnp.ones((slots, 128), BF))
        free = jnp.concatenate([jnp.where(served > 0, 0.0, 1.0)] * (width // 256), axis=1)
        base_ref[at, :] = (mem_ref[at, cols].astype(F32) * free).astype(BF)
        base_ref.send(part)


def part_of(ref, packed, start, size):
    if packed:
        return ref[:, start : start + size, :].reshape(-1, ref.shape[2])
    return ref[...]


def message_part(own, pack_ref, first, half):
    slots = pack_ref.shape[0]
    at_count, at_pre, at_weight, at_sent, _ = pack_places(slots, half)
    both = dot(own, pack_ref[first : first + half, at_weight:at_sent])
    count = pack_ref[:, at_count:at_pre].astype(F32)
    count = jnp.concatenate([count] * (half // 128), axis=1)
    return dot(pack_ref[:, :at_count], both[:, :half].astype(BF)) + count * both[:, half:]


def own_message_kernel(packed, cap, cap_self, own_ref, pack_ref, total_ref):
    half = own_ref.shape[-1]
    _, at_pre, at_weight, _, _ = pack_places(pack_ref.shape[0], half)
    pre = pack_ref[:, at_pre : at_pre + half].astype(F32)
    pre = pre + pack_ref[:, at_pre + half : at_weight].astype(F32)
    own = part_of(own_ref, packed, cap, cap_self)
    total_ref[...] = message_part(own, pack_ref, 0, half) + pre


def message_kernel(packed, peers, cap, cap_self, oth_ref, pack_ref, total_ref, out_ref):
    half = oth_ref.shape[-1]
    at_sent = pack_places(pack_ref.shape[0], half)[3]
    oth = part_of(oth_ref, packed, cap, cap_self)
    out = total_ref[...] + message_part(oth, pack_ref, half, half)
    if not packed:
        out_ref[...] = out.astype(BF)
        return
    parts = out.reshape(peers, cap_self // 8, 8, half)
    parts = [parts[:, n] for n in range(cap_self // 8)]
    parts.append(jnp.broadcast_to(pack_ref[:peers, at_sent:].astype(F32)[:, None, :], (peers, 8, 128)))
    out_ref[...] = jnp.concatenate(parts, axis=2).astype(BF)


def attention_kernel(
    packed,
    cap,
    cap_self,
    *refs,
):
    own_refs, oth_refs, refs = (refs[:1], refs[1:2], refs[2:]) if packed else (
        refs[:2], refs[2:4], refs[4:]
    )
    wkvt_ref, nslot_ref, te_ref, wqt_ref, slot_t_ref, phase_ref, wout_ref, wself_ref = refs[:8]
    emb_ref, kv_w, value_ref = refs[8:]
    nown_ref, sown_ref = own_refs[0], own_refs[-1]
    noth_ref, soth_ref = oth_refs[0], oth_refs[-1]
    core = lax.axis_index("mp")
    half = wout_ref.shape[0]
    width = 2 * half
    size = width // HEADS
    heads = HEADS // 2
    mine, theirs = half_of(core, half), half_of(1 - core, half)
    fown = part_of(nown_ref, packed, 0, cap)
    foth = part_of(noth_ref, packed, 0, cap)
    for ref in (te_ref, wout_ref, wself_ref):
        ref.start()
    slots = fown.shape[0]
    kv_w[:, :slots] = (dot_nt(wkvt_ref[:, mine], fown) + dot_nt(wkvt_ref[:, theirs], foth)).astype(BF)
    kv_w[:, slots:] = wkvt_ref[:, width:]
    xown = part_of(sown_ref, packed, cap, cap_self)
    xoth = part_of(soth_ref, packed, cap, cap_self)
    slots_s = xown.shape[0]
    te_self = encode_turns(phase_ref[...]).astype(BF)
    te_self = jnp.broadcast_to(te_self, (128, te_self.shape[1]))
    query = dot_nt(wqt_ref[:, mine], xown) + dot_nt(wqt_ref[:, theirs], xoth)
    query_te = dot_nt(wqt_ref[:, width:], te_self)
    query = (query + jnp.concatenate([query_te] * (slots_s // 128), axis=1)).astype(BF)
    find = jnp.concatenate(tall_one_hot(slot_t_ref, slots_s), axis=1)
    q = dot(query, find) * (1.0 / size**0.5)
    neigh, _, ends = te_ref.shape
    at = lax.broadcasted_iota(jnp.int16, (slots, ends), 0)
    one, zero = jnp.ones((), BF), jnp.zeros((), BF)
    weights = []
    for k in range(neigh):
        line = jnp.concatenate([nslot_ref[j, k : k + 1, :] for j in range(2)], axis=1)
        line = jnp.broadcast_to(line, (16, ends)).astype(jnp.int16)
        line = jnp.concatenate([line] * (slots // 16), axis=0)
        hot = jnp.where(at == line, one, zero)
        right = jnp.concatenate([hot, te_ref[k]], axis=0)
        kv = dot(kv_w[...], right)
        value_ref[k] = kv[half:].astype(BF)
        score = q * kv[:half]
        score = [
            jnp.sum(score[h * size : (h + 1) * size], axis=0, keepdims=True) for h in range(heads)
        ]
        weights.append(jnp.exp(jnp.concatenate(score, axis=0)))
    total = weights[0]
    for k in range(1, neigh):
        total = total + weights[k]
    weights = [(w / total).astype(BF).astype(F32) for w in weights]
    att = []
    for h in range(heads):
        part = jnp.zeros((size, ends), F32)
        for k in range(neigh):
            value = value_ref[k, h * size : (h + 1) * size, :].astype(F32)
            part = part + weights[k][h : h + 1] * value
        att.append(part)
    att = jnp.concatenate(att, axis=0).T.astype(BF)
    events = ends // 2
    at = iota((events, slots_s), 1)
    find = [
        one_hot(at == down(slot_t_ref[j : j + 1, :].astype(F32), slots_s).astype(I32))
        for j in range(2)
    ]
    self_own = dot(jnp.concatenate(find, axis=0), xown).astype(BF)
    emb_ref[...] = (dot(att, wout_ref[...]) + dot(self_own, wself_ref[...])).astype(BF)


def sum_kernel(own_ref, oth_ref, out_ref):
    total = own_ref[...].astype(F32) + oth_ref[...].astype(F32)
    events = out_ref.shape[0]
    out_ref[...] = jnp.stack([total[:events], total[events:]], axis=1).astype(BF)


def update_kernel(
    packed,
    cap_self,
    own_ref,
    oth_ref,
    count_ref,
    serve_ref,
    win_ref,
    gh_ref,
    old_ref,
    base_ref,
    out_ref,
    put,
):
    core = lax.axis_index("mp")
    rows, half = base_ref.shape
    serve = serve_ref[0]
    slots = serve.size

    def messages(ref):
        if not packed:
            return ref[...]
        values = ref[...].astype(F32)
        parts = [
            values[:, None, :, n * half : (n + 1) * half] for n in range(cap_self // 8)
        ]
        return jnp.concatenate(parts, axis=1).reshape(slots, half).astype(BF)

    line = row(serve)
    match = column(serve, 0, slots) == line
    same = one_hot(match)
    earlier = match & (iota((slots, slots), 0) < iota((slots, slots), 1))
    again = jnp.sum(jnp.where(earlier, 1.0, 0.0), axis=0, keepdims=True)
    line = jnp.where(again > 0, -1.0, line)
    step = rows // out_ref.parts
    for part in range(out_ref.parts):
        put[part * step : (part + 1) * step, :] = hot_rows(line, part * step, step)
    peers = slots // cap_self
    counts = count_ref[...]
    if packed:
        counts = counts.astype(F32)[:, 0, counts.shape[2] - 128 :].astype(BF)
    spread = dot(one_hot(iota((slots, peers), 0) // cap_self == iota((slots, peers), 1)), counts)
    lane = iota((slots, 128), 1)
    spread = jnp.where(iota((slots, 128), 0) % cap_self == lane, spread, 0.0).astype(BF)
    count = jnp.sum(dot(same, spread), axis=1, keepdims=True)
    inverse = 1.0 / jnp.maximum(count, 1.0)
    own = (dot(same, messages(own_ref)) * inverse).astype(BF)
    oth = (dot(same, messages(oth_ref)) * inverse).astype(BF)
    mine, theirs = half_of(core, half), half_of(1 - core, half)
    gi = [dot(own, win_ref[g, mine, :]) + dot(oth, win_ref[g, theirs, :]) for g in range(3)]
    reset = jax.nn.sigmoid(gi[0] + gh_ref[0])
    gate = jax.nn.sigmoid(gi[1] + gh_ref[1])
    cand = jnp.tanh(gi[2] + reset * gh_ref[2])
    old = old_ref[...].reshape(slots, half).astype(F32)
    fresh = jnp.where(count > 0, (1.0 - gate) * cand + gate * old, old).astype(BF)
    for part in range(out_ref.parts):
        at = slice(part * step, (part + 1) * step)
        moved = dot(put[at, :], fresh)
        out_ref[at, :] = (base_ref[at, :].astype(F32) + moved).astype(BF)
        out_ref.send(part)


def per_device(
    memory,
    ev_time,
    nbr_time,
    edge_feat,
    self_slot,
    nbr_slot,
    serve_self,
    serve_rows,
    freq,
    phase,
    w_query,
    w_key,
    w_value,
    w_out,
    w_self,
    w_msg_self,
    w_msg_other,
    w_msg_time,
    w_msg_edge,
    w_in,
    w_hid,
):
    owned, width = memory.shape
    half = w_out.shape[0]
    peers, cap = serve_rows.shape[1:]
    cap_self = serve_self.shape[2]
    events, _, neigh = nbr_slot.shape
    ends = 2 * events
    tdim = freq.shape[0]
    slots_n, slots_s = peers * cap, peers * cap_self
    packed = cap % 16 == 0 and cap_self % 16 == 0
    shape = jax.ShapeDtypeStruct

    core = lax.axis_index("mp")

    def call(kernel, out_shape, args, flops=0, scratch=(), limit=62, direct=(), views={}, parts=(), small=False, late=()):
        single = not isinstance(out_shape, (list, tuple))
        outs = [out_shape] if single else list(out_shape)
        parts = [*parts, *[1] * (len(outs) - len(parts))]
        size = sum(a.size * a.dtype.itemsize for a in (*args, *outs))
        whole, rooms = [], []
        for n, arg in enumerate(args):
            if n in direct:
                whole.append(None)
                continue
            view, room = views.get(n, (lambda ref: ref, arg.shape))
            whole.append(view)
            rooms.append(pltpu.VMEM(room, arg.dtype))
        rooms += [pltpu.VMEM(o.shape, o.dtype) for o in outs]
        return pl.pallas_call(
            functools.partial(staged, kernel, whole, parts, late),
            out_shape=out_shape,
            in_specs=[HBM if view else VMEM for view in whole],
            out_specs=HBM if single else [HBM] * len(outs),
            scratch_shapes=[
                *rooms,
                *scratch,
                pltpu.SemaphoreType.DMA((len(args),)),
                pltpu.SemaphoreType.DMA((len(outs), max(parts))),
            ],
            compiler_params=pltpu.CompilerParams(vmem_limit_bytes=limit * 1024 * 1024),
            cost_estimate=pl.CostEstimate(
                flops=int(flops), bytes_accessed=1 if small else int(size), transcendentals=0
            ),
        )(*args)

    def plain(kernel, out_shape, args, flops, limit):
        size = sum(a.size * a.dtype.itemsize for a in (*args, out_shape))
        return pl.pallas_call(
            kernel,
            out_shape=out_shape,
            in_specs=[VMEM] * len(args),
            out_specs=VMEM,
            compiler_params=pltpu.CompilerParams(vmem_limit_bytes=limit * 1024 * 1024),
            cost_estimate=pl.CostEstimate(
                flops=int(flops), bytes_accessed=int(size), transcendentals=0
            ),
        )(*args)

    def columns(rows):
        return (lambda ref: ref.at[:, half_of(lax.axis_index("mp"), half)], (rows, half))

    def stripe(part, size):
        return (
            lambda ref: ref.at[pl.ds(part * size, size), half_of(lax.axis_index("mp"), half)],
            (size, half),
        )

    def swap(x):
        return lax.ppermute(x, "mp", [(0, 1), (1, 0)])

    def exchange(x):
        return lax.all_to_all(x, "nodes", split_axis=0, concat_axis=0, tiled=True)

    flops_serve = 2 * (slots_n + slots_s) * owned * half
    if packed:
        served_shape = shape((peers, cap + cap_self, half), BF)
    else:
        served_shape = [shape((slots_n, half), BF), shape((slots_s, half), BF)]
    quarter = owned
    served = call(
        functools.partial(serve_kernel, packed),
        served_shape,
        (serve_rows, serve_self, memory),
        flops_serve,
        [pltpu.VMEM((1024, owned), BF)],
        views={2 + n: stripe(n, quarter) for n in range(1)},
        parts=[slots_s // 256] if packed and cap == cap_self else (),
    )
    if packed:
        old = served
        old_view = (lambda ref: ref.at[:, pl.ds(cap, cap_self), :], (peers, cap_self, half))
    else:
        served_n, old = served
        old_view = (lambda ref: ref, old.shape)
        served = jnp.concatenate(
            [served_n.reshape(peers, cap, half), old.reshape(peers, cap_self, half)], axis=1
        )
    fetched = exchange(served)

    away = lax.dynamic_slice_in_dim(
        jnp.concatenate([w_msg_self, w_msg_other, w_msg_time, w_msg_edge], axis=0),
        (1 - core) * half,
        half,
        1,
    )
    w_swap = swap(away)
    edge_t = edge_feat.T
    edge_swap = swap(edge_t)
    nslot = nbr_slot.transpose(1, 2, 0)
    slot_t = self_slot.T
    gh, te, wq_t, wkv_t, base = call(
        prepare_kernel,
        [
            shape((3, slots_s, half), F32),
            shape((neigh, tdim, ends), BF),
            shape((half, width + tdim), BF),
            shape((2 * half, width + tdim), BF),
            shape((owned, half), BF),
        ],
        (
            serve_self,
            ev_time[None],
            nbr_time.transpose(1, 2, 0),
            freq[None],
            phase[None],
            memory,
            w_hid.transpose(1, 0, 2),
            w_query,
            w_key,
            w_value,
        ),
        2 * slots_s * (owned * width + width * 3 * half),
        parts=[1, 1, 1, 1, 8],
    )
    tpart = w_msg_time.shape[0]
    pack = call(
        functools.partial(slot_kernel, peers),
        shape((slots_s, pack_places(slots_s, half)[-1]), BF),
        (
            slot_t,
            te,
            edge_t,
            edge_swap,
            w_msg_time,
            w_msg_edge,
            w_msg_self,
            w_msg_other,
            w_swap,
        ),
        4 * slots_s * events * (slots_s + half),
        limit=50,
        views={
            1: (lambda ref: ref.at[pl.ds(0, 1)], (1, tdim, ends)),
            4: columns(tpart),
            5: columns(w_msg_edge.shape[0]),
            6: columns(half),
            7: columns(half),
        },
    )
    fetched, te, pack, gh, base = lax.optimization_barrier((fetched, te, pack, gh, base))
    fetched_x = swap(fetched)
    if packed:
        both = (fetched, fetched_x)
        mine = (fetched, fetched_x)
        back_shape = shape((peers, 8, cap_self // 8 * half + 128), BF)
    else:
        nbr = [f[:, :cap].reshape(slots_n, half) for f in (fetched, fetched_x)]
        mine = [f[:, cap:].reshape(slots_s, half) for f in (fetched, fetched_x)]
        both = (nbr[0], mine[0], nbr[1], mine[1])
        back_shape = shape((slots_s, half), BF)
    total = plain(
        functools.partial(own_message_kernel, packed, cap, cap_self),
        shape((slots_s, half), F32),
        (mine[0], pack),
        slots_s * half * (2 * width + slots_s),
        50,
    )
    message = plain(
        functools.partial(message_kernel, packed, peers, cap, cap_self),
        back_shape,
        (mine[1], pack, total),
        slots_s * half * (2 * width + slots_s),
        50,
    )
    message, slot_t2 = lax.optimization_barrier((message, slot_t))
    part = call(
        functools.partial(attention_kernel, packed, cap, cap_self),
        shape((ends, width), BF),
        (*both, wkv_t, nslot, te, wq_t, slot_t2, phase[None], w_out, w_self),
        2 * ends * neigh * (slots_n + tdim) * width,
        [pltpu.VMEM((2 * half, slots_n + tdim), BF), pltpu.VMEM((neigh, half, ends), BF)],
        direct=range(len(both)),
        late=[len(both) + n for n in (2, 6, 7)],
        limit=53,
    )
    embedding = call(
        sum_kernel, shape((events, 2, width), BF), (part, swap(part)), direct=(0, 1), small=True, limit=52
    )
    if not packed:
        message = jnp.concatenate(
            [
                message.reshape(peers, cap_self, half),
                jnp.pad(pack[:peers, -128:], ((0, 0), (0, half - 128)))[:, None],
            ],
            axis=1,
        )
    back = exchange(message)
    back, embedding = lax.optimization_barrier((back, embedding))
    back_x = swap(back)
    counts = back
    if not packed:
        back_x = back_x[:, :cap_self].reshape(slots_s, half)
        counts = back[:, cap_self, :128]
        back = back[:, :cap_self].reshape(slots_s, half)
    memory_out = call(
        functools.partial(update_kernel, packed, cap_self),
        shape((owned, half), BF),
        (back, back_x, counts, serve_self, w_in.transpose(1, 0, 2), gh, old, base),
        2 * slots_s * (slots_s * width + width * 3 * half + owned * half),
        [pltpu.VMEM((owned, slots_s), BF)],
        direct=(0, 1, 2),
        views={6: old_view},
        parts=[8],
        limit=53,
    )
    return (embedding, memory_out)


def solution(mesh):
    return jax.shard_map(
        per_device,
        mesh=mesh,
        in_specs=(
            P("nodes", None),
            P("nodes"),
            P("nodes", None, None),
            P("nodes", "mp"),
            P("nodes", None),
            P("nodes", None, None),
            P("nodes", None, None),
            P("nodes", None, None),
            P(),
            P(),
            P(None, "mp"),
            P(None, "mp"),
            P(None, "mp"),
            P("mp", None),
            P("mp", None),
            P("mp", None),
            P("mp", None),
            P("mp", None),
            P("mp", None),
            P(None, None, "mp"),
            P(None, None, "mp"),
        ),
        out_specs=(P("nodes", None, None), P("nodes", "mp")),
        check_vma=False,
    )
```

```python
import functools

import jax
import jax.numpy as jnp
from jax import lax
from jax.experimental import pallas as pl
from jax.experimental.pallas import tpu as pltpu
from jax.sharding import PartitionSpec as P

HEADS = 8
BF = jnp.bfloat16
F32 = jnp.float32
I32 = jnp.int32
VMEM = pl.BlockSpec(memory_space=pltpu.VMEM)
HBM = pl.BlockSpec(memory_space=pltpu.HBM)
TURN = 6.283185307179586
COS = (
    6.52861337,
    -25.9675685,
    60.1676231,
    -85.4501386,
    64.9391174,
    -19.7392045,
    0.999999989,
)


def dot(a, b):
    return jnp.dot(a, b, preferred_element_type=F32)


def dot_nt(a, b):
    return lax.dot_general(a, b, (((1,), (1,)), ((), ())), preferred_element_type=F32)


def iota(shape, dim):
    return lax.broadcasted_iota(I32, shape, dim)


class Operand:
    def __init__(self, copy, ref):
        self.copy, self.ref, self.shape = copy, ref, ref.shape
        self.started = False

    def start(self):
        if not self.started:
            self.copy.start()
            self.started = True

    def wait(self):
        if self.copy is not None:
            self.start()
            self.copy.wait()
            self.copy = None

    def __getitem__(self, at):
        self.wait()
        return self.ref[at]


class Result:
    def __init__(self, room, ref, sems, parts):
        self.room, self.ref, self.sems, self.parts = room, ref, sems, parts
        self.shape, self.sent = room.shape, []

    def __setitem__(self, at, value):
        self.room[at] = value

    def __getitem__(self, at):
        return self.room[at]

    def send(self, part):
        size = self.shape[0] // self.parts
        at = pl.ds(part * size, size)
        copy = pltpu.make_async_copy(self.room.at[at], self.ref.at[at], self.sems.at[part])
        copy.start()
        self.sent.append((part, copy))

    def finish(self):
        done = [part for part, _ in self.sent]
        for part in range(self.parts):
            if part not in done:
                self.send(part)
        for _, copy in self.sent:
            copy.wait()


def staged(kernel, views, parts, late, *refs):
    count, outs = len(views), len(parts)
    ins, results, rest = refs[:count], refs[count : count + outs], list(refs[count + outs :])
    in_sems, out_sems = rest[-2:]
    rest = rest[:-2]
    operands = []
    for n, (ref, view) in enumerate(zip(ins, views)):
        if view is None:
            operands.append(ref)
        else:
            room = rest.pop(0)
            operands.append(Operand(pltpu.make_async_copy(view(ref), room, in_sems.at[n]), room))
    for n, operand in enumerate(operands):
        if isinstance(operand, Operand) and n not in late:
            operand.start()
    held = [
        Result(rest.pop(0), ref, out_sems.at[n], part)
        for n, (ref, part) in enumerate(zip(results, parts))
    ]
    kernel(*operands, *held, *rest)
    for operand in operands:
        if isinstance(operand, Operand):
            operand.wait()
    for result in held:
        result.finish()


def one_hot(mask):
    return jnp.where(mask, 1.0, 0.0).astype(BF)


def split(serve):
    high = lax.shift_right_logical(serve, 8)
    low = jnp.bitwise_and(serve, 255)
    return high.astype(F32).astype(BF), low.astype(F32).astype(BF)


def column(serve, start, count):
    peers, cap = serve.shape
    high, low = split(serve)
    pick = one_hot((iota((count, peers), 0) + start) // cap == iota((count, peers), 1))
    every = 256.0 * dot(pick, high) + dot(pick, low)
    mine = (iota((count, cap), 0) + start) % cap == iota((count, cap), 1)
    return jnp.sum(jnp.where(mine, every, 0.0), axis=1, keepdims=True)


def row(serve):
    peers, cap = serve.shape
    slots = peers * cap
    high, low = split(serve)
    pick = one_hot(iota((cap, slots), 1) % cap == iota((cap, slots), 0))
    every = 256.0 * dot(high, pick) + dot(low, pick)
    mine = iota((peers, slots), 1) // cap == iota((peers, slots), 0)
    return jnp.sum(jnp.where(mine, every, 0.0), axis=0, keepdims=True)


def hot_rows(line, start, count):
    width = line.shape[1]
    near = (line - start).astype(I32)
    near = jnp.where((near >= 0) & (near < count), near, -1)
    near = jnp.broadcast_to(near, (16, width)).astype(jnp.int16)
    near = jnp.concatenate([near] * (count // 16), axis=0)
    at = lax.broadcasted_iota(jnp.int16, (count, width), 0)
    return jnp.where(at == near, jnp.ones((), BF), jnp.zeros((), BF))


def rows_at(col, count):
    near = jnp.broadcast_to(col, (col.shape[0], 128)).astype(I32).astype(jnp.int16)
    near = jnp.concatenate([near] * (count // 128), axis=1)
    at = lax.broadcasted_iota(jnp.int16, near.shape, 1)
    return jnp.where(at == near, jnp.ones((), BF), jnp.zeros((), BF))


def half_of(core, half):
    return pl.ds(pl.multiple_of(core * half, half), half)


def serve_kernel(packed, rows_ref, self_ref, *refs):
    mems, outs, hot = refs[:1], refs[1:-1], refs[-1]
    depth, half = mems[0].shape
    count = len(mems) * depth
    step = 256
    rows, own = rows_ref[0], self_ref[0]
    jobs = []
    for table, serve in enumerate((rows, own)):
        jobs += [(start, table, serve) for start in range(0, serve.size, step)]
    jobs.sort(key=lambda job: (job[0], job[1]))
    early = hot.shape[0] // step
    for n, (start, table, serve) in enumerate(jobs[:early]):
        hot[n * step : (n + 1) * step, :] = rows_at(column(serve, start, step), count)
    for n, (start, table, serve) in enumerate(jobs):
        if n < early:
            at = hot[n * step : (n + 1) * step, :]
        else:
            at = rows_at(column(serve, start, step), count)
        picked = dot(at[:, :depth], mems[0][...])
        for part in range(1, len(mems)):
            picked = picked + dot(at[:, part * depth : (part + 1) * depth], mems[part][...])
        picked = picked.astype(BF)
        if packed:
            cap = serve.shape[1]
            first = table * rows.shape[1]
            outs[0][start // cap : (start + step) // cap, first : first + cap, :] = picked.reshape(
                step // cap, cap, half
            )
            if outs[0].parts > 1 and table == 1:
                outs[0].send(start // step)
        else:
            outs[table][start : start + step, :] = picked


def encode_turns(x):
    turns = x * (1.0 / TURN)
    u = turns - jnp.round(turns)
    square = u * u
    total = jnp.full_like(square, COS[0])
    for factor in COS[1:]:
        total = total * square + factor
    return total


def down(line, count):
    return jnp.broadcast_to(line, (count, line.shape[1])).T


def time_kernel(
    ev_ref, nbr_ref, freq_ref, phase_ref, wq_ref, wk_ref, wv_ref, te_ref, wqt_ref, wkvt_ref, kvte_ref
):
    neigh, ends = kvte_ref.shape[0] - 3, kvte_ref.shape[2]
    tdim = te_ref.shape[1]
    events = ends // 2
    freq = down(freq_ref[...], events)
    phase = down(phase_ref[...], events)
    time = ev_ref[...]
    half = wq_ref.shape[1]
    wqt_ref[...] = wq_ref[...].T
    wkvt_ref[:half, :] = wk_ref[...].T
    wkvt_ref[half:, :] = wv_ref[...].T
    wqt_ref.send(0)
    wkvt_ref.send(0)
    weight = wkvt_ref[:, wkvt_ref.shape[1] - tdim :]
    for k in range(neigh):
        enc = []
        for j in range(2):
            delta = (time - nbr_ref[j, k : k + 1, :]).astype(F32)
            enc.append(encode_turns(delta * freq + phase).astype(BF))
        enc = jnp.concatenate(enc, axis=1)
        if k == 0:
            te_ref[0] = enc
        kvte_ref[k] = dot(weight, enc).astype(BF)
        kvte_ref.send(k)


def tall_one_hot(slot_t_ref, slots):
    events = slot_t_ref.shape[1]
    at = iota((slots, events), 0)
    return [one_hot(at == slot_t_ref[j : j + 1, :]) for j in range(2)]


def pack_places(slots, half):
    at_pre = slots + 128
    at_weight = at_pre + 2 * half
    at_sent = at_weight + 2 * half
    return slots, at_pre, at_weight, at_sent, at_sent + 128


def slot_kernel(
    peers,
    slot_t_ref,
    te_ref,
    edge_ref,
    edge_x_ref,
    wt_ref,
    we_ref,
    ws_ref,
    wo_ref,
    wx_ref,
    pack_ref,
):
    core = lax.axis_index("mp")
    slots = pack_ref.shape[0]
    part, half = wt_ref.shape
    tall = tall_one_hot(slot_t_ref, slots)
    events = tall[0].shape[1]
    both = tall[0] + tall[1]
    at_count, at_pre, at_weight, at_sent = pack_places(slots, half)[:4]
    pack_ref[:, :at_count] = (dot_nt(tall[0], tall[1]) + dot_nt(tall[1], tall[0])).astype(BF)
    count = dot_nt(both, jnp.ones((128, events), BF))
    pack_ref[:, at_count:at_pre] = count.astype(BF)
    cap = slots // peers
    place = iota((slots, 128), 0) % cap == iota((slots, 128), 1)
    owner = one_hot(iota((peers, slots), 1) // cap == iota((peers, slots), 0))
    pack_ref[:peers, at_sent:] = dot(owner, jnp.where(place, count, 0.0).astype(BF)).astype(BF)
    pack_ref[peers:, at_sent:] = jnp.zeros((slots - peers, 128), BF)
    pack_ref[:half, at_weight : at_weight + half] = wo_ref[...]
    pack_ref[:half, at_weight + half : at_sent] = ws_ref[...]
    pack_ref[half : 2 * half, at_weight : at_weight + half] = wx_ref[half : 2 * half, :]
    pack_ref[half : 2 * half, at_weight + half : at_sent] = wx_ref[:half, :]
    mine, theirs = wt_ref[...], wx_ref[2 * half : 2 * half + part, :]
    first = core == 0
    weight = jnp.concatenate(
        [
            jnp.where(first, mine, theirs),
            jnp.where(first, theirs, mine),
            we_ref[...],
            wx_ref[2 * half + part :, :],
        ],
        axis=0,
    )
    edge = jnp.concatenate([edge_ref[...], edge_x_ref[...]], axis=0)
    value = jnp.concatenate(
        [dot_nt(jnp.concatenate(tall, axis=1), te_ref[0]), dot_nt(both, edge)], axis=1
    )
    high = value.astype(BF)
    low = (value - high.astype(F32)).astype(BF)
    pre = dot(high, weight) + dot(low, weight)
    high = pre.astype(BF)
    pack_ref[:, at_pre : at_pre + half] = high
    pack_ref[:, at_pre + half : at_weight] = (pre - high.astype(F32)).astype(BF)


def prepare_kernel(
    self_ref,
    ev_ref,
    nbr_ref,
    freq_ref,
    phase_ref,
    mem_ref,
    whid_ref,
    wq_ref,
    wk_ref,
    wv_ref,
    win_ref,
    gh_ref,
    te_ref,
    wqt_ref,
    wkvt_ref,
    base_ref,
    kvte_ref,
):
    time_kernel(
        ev_ref, nbr_ref, freq_ref, phase_ref, wq_ref, wk_ref, wv_ref, te_ref, wqt_ref, wkvt_ref, kvte_ref
    )
    te_ref.send(0)
    planes = kvte_ref.shape[0]
    for g in range(3):
        kvte_ref[planes - 3 + g] = win_ref[g]
        kvte_ref.send(planes - 3 + g)
    count, width = mem_ref.shape
    serve = self_ref[0]
    slots = serve.size
    col = column(serve, 0, slots)
    for start in range(0, slots, 256):
        at = slice(start, start + 256)
        picked = dot(rows_at(col[at], count), mem_ref[...]).astype(BF)
        for g in range(3):
            gh_ref[g, at, :] = dot(picked, whid_ref[g])
    gh_ref.send(0)
    line = row(serve)
    cols = half_of(lax.axis_index("mp"), width // 2)
    step = count // base_ref.parts
    for part in range(base_ref.parts):
        at = slice(part * step, (part + 1) * step)
        hit = hot_rows(line, part * step, step)
        served = dot(hit, jnp.ones((slots, 128), BF))
        free = jnp.concatenate([jnp.where(served > 0, 0.0, 1.0)] * (width // 256), axis=1)
        base_ref[at, :] = (mem_ref[at, cols].astype(F32) * free).astype(BF)
        base_ref.send(part)


def part_of(ref, packed, start, size):
    if packed:
        return ref[:, start : start + size, :].reshape(-1, ref.shape[2])
    return ref[...]


def message_part(own, pack_ref, first, half):
    slots = pack_ref.shape[0]
    at_count, at_pre, at_weight, at_sent, _ = pack_places(slots, half)
    both = dot(own, pack_ref[first : first + half, at_weight:at_sent])
    count = pack_ref[:, at_count:at_pre].astype(F32)
    count = jnp.concatenate([count] * (half // 128), axis=1)
    return dot(pack_ref[:, :at_count], both[:, :half].astype(BF)) + count * both[:, half:]


def own_message_kernel(packed, cap, cap_self, own_ref, pack_ref, total_ref):
    half = own_ref.shape[-1]
    _, at_pre, at_weight, _, _ = pack_places(pack_ref.shape[0], half)
    pre = pack_ref[:, at_pre : at_pre + half].astype(F32)
    pre = pre + pack_ref[:, at_pre + half : at_weight].astype(F32)
    own = part_of(own_ref, packed, cap, cap_self)
    total_ref[...] = message_part(own, pack_ref, 0, half) + pre


def message_kernel(packed, peers, cap, cap_self, oth_ref, pack_ref, total_ref, out_ref):
    half = oth_ref.shape[-1]
    at_sent = pack_places(pack_ref.shape[0], half)[3]
    oth = part_of(oth_ref, packed, cap, cap_self)
    out = total_ref[...] + message_part(oth, pack_ref, half, half)
    if not packed:
        out_ref[...] = out.astype(BF)
        return
    parts = out.reshape(peers, cap_self // 8, 8, half)
    parts = [parts[:, n] for n in range(cap_self // 8)]
    parts.append(jnp.broadcast_to(pack_ref[:peers, at_sent:].astype(F32)[:, None, :], (peers, 8, 128)))
    out_ref[...] = jnp.concatenate(parts, axis=2).astype(BF)


def attention_kernel(
    packed,
    cap,
    cap_self,
    *refs,
):
    own_refs, oth_refs, refs = (refs[:1], refs[1:2], refs[2:]) if packed else (
        refs[:2], refs[2:4], refs[4:]
    )
    wkvt_ref, nslot_ref, wqt_ref, slot_t_ref, phase_ref, wout_ref, wself_ref = refs[:7]
    te_refs, (emb_ref, kv_w, value_ref) = refs[7:-3], refs[-3:]
    nown_ref, sown_ref = own_refs[0], own_refs[-1]
    noth_ref, soth_ref = oth_refs[0], oth_refs[-1]
    core = lax.axis_index("mp")
    half = wout_ref.shape[0]
    width = 2 * half
    size = width // HEADS
    heads = HEADS // 2
    mine, theirs = half_of(core, half), half_of(1 - core, half)
    fown = part_of(nown_ref, packed, 0, cap)
    foth = part_of(noth_ref, packed, 0, cap)
    for ref in (*te_refs, wout_ref, wself_ref):
        ref.start()
    slots = fown.shape[0]
    kv_w[...] = (dot_nt(wkvt_ref[:, mine], fown) + dot_nt(wkvt_ref[:, theirs], foth)).astype(BF)
    xown = part_of(sown_ref, packed, cap, cap_self)
    xoth = part_of(soth_ref, packed, cap, cap_self)
    slots_s = xown.shape[0]
    te_self = encode_turns(phase_ref[...]).astype(BF)
    te_self = jnp.broadcast_to(te_self, (128, te_self.shape[1]))
    query = dot_nt(wqt_ref[:, mine], xown) + dot_nt(wqt_ref[:, theirs], xoth)
    query_te = dot_nt(wqt_ref[:, width:], te_self)
    query = (query + jnp.concatenate([query_te] * (slots_s // 128), axis=1)).astype(BF)
    find = jnp.concatenate(tall_one_hot(slot_t_ref, slots_s), axis=1)
    q = dot(query, find) * (1.0 / size**0.5)
    neigh, depth = nslot_ref.shape[1], te_refs[0].shape[0]
    ends = te_refs[0].shape[2]
    at = lax.broadcasted_iota(jnp.int16, (slots, ends), 0)
    one, zero = jnp.ones((), BF), jnp.zeros((), BF)
    weights = []
    for k in range(neigh):
        line = jnp.concatenate([nslot_ref[j, k : k + 1, :] for j in range(2)], axis=1)
        line = jnp.broadcast_to(line, (16, ends)).astype(jnp.int16)
        line = jnp.concatenate([line] * (slots // 16), axis=0)
        hot = jnp.where(at == line, one, zero)
        kv = dot(kv_w[...], hot) + te_refs[k // depth][k % depth].astype(F32)
        value_ref[k] = kv[half:].astype(BF)
        score = q * kv[:half]
        score = [
            jnp.sum(score[h * size : (h + 1) * size], axis=0, keepdims=True) for h in range(heads)
        ]
        weights.append(jnp.exp(jnp.concatenate(score, axis=0)))
    total = weights[0]
    for k in range(1, neigh):
        total = total + weights[k]
    weights = [(w / total).astype(BF).astype(F32) for w in weights]
    att = []
    for h in range(heads):
        part = jnp.zeros((size, ends), F32)
        for k in range(neigh):
            value = value_ref[k, h * size : (h + 1) * size, :].astype(F32)
            part = part + weights[k][h : h + 1] * value
        att.append(part)
    att = jnp.concatenate(att, axis=0).T.astype(BF)
    events = ends // 2
    at = iota((events, slots_s), 1)
    find = [
        one_hot(at == down(slot_t_ref[j : j + 1, :].astype(F32), slots_s).astype(I32))
        for j in range(2)
    ]
    self_own = dot(jnp.concatenate(find, axis=0), xown).astype(BF)
    emb_ref[...] = (dot(att, wout_ref[...]) + dot(self_own, wself_ref[...])).astype(BF)


def sum_kernel(own_ref, oth_ref, _, out_ref):
    total = own_ref[...].astype(F32) + oth_ref[...].astype(F32)
    events = out_ref.shape[0]
    out_ref[...] = jnp.stack([total[:events], total[events:]], axis=1).astype(BF)


def touch_kernel(*refs):
    refs[-1][...] = sum(
        (ref[:8, :128] if len(ref.shape) == 2 else ref[0, :8, :128]).astype(F32)
        for ref in refs[:-1]
    )


def update_kernel(
    packed,
    cap_self,
    own_ref,
    oth_ref,
    count_ref,
    serve_ref,
    win_ref,
    gh_ref,
    old_ref,
    base_ref,
    out_ref,
    put,
):
    core = lax.axis_index("mp")
    rows, half = base_ref.shape
    serve = serve_ref[0]
    slots = serve.size

    def messages(ref):
        if not packed:
            return ref[...]
        values = ref[...].astype(F32)
        parts = [
            values[:, None, :, n * half : (n + 1) * half] for n in range(cap_self // 8)
        ]
        return jnp.concatenate(parts, axis=1).reshape(slots, half).astype(BF)

    line = row(serve)
    match = column(serve, 0, slots) == line
    same = one_hot(match)
    earlier = match & (iota((slots, slots), 0) < iota((slots, slots), 1))
    again = jnp.sum(jnp.where(earlier, 1.0, 0.0), axis=0, keepdims=True)
    line = jnp.where(again > 0, -1.0, line)
    step = rows // out_ref.parts
    for part in range(out_ref.parts):
        put[part * step : (part + 1) * step, :] = hot_rows(line, part * step, step)
    peers = slots // cap_self
    counts = count_ref[...]
    if packed:
        counts = counts.astype(F32)[:, 0, counts.shape[2] - 128 :].astype(BF)
    spread = dot(one_hot(iota((slots, peers), 0) // cap_self == iota((slots, peers), 1)), counts)
    lane = iota((slots, 128), 1)
    spread = jnp.where(iota((slots, 128), 0) % cap_self == lane, spread, 0.0).astype(BF)
    count = jnp.sum(dot(same, spread), axis=1, keepdims=True)
    inverse = 1.0 / jnp.maximum(count, 1.0)
    own = (dot(same, messages(own_ref)) * inverse).astype(BF)
    oth = (dot(same, messages(oth_ref)) * inverse).astype(BF)
    mine, theirs = half_of(core, half), half_of(1 - core, half)
    gi = [dot(own, win_ref[g, mine, :]) + dot(oth, win_ref[g, theirs, :]) for g in range(3)]
    reset = jax.nn.sigmoid(gi[0] + gh_ref[0])
    gate = jax.nn.sigmoid(gi[1] + gh_ref[1])
    cand = jnp.tanh(gi[2] + reset * gh_ref[2])
    old = part_of(old_ref, packed, old_ref.shape[1] - cap_self, cap_self).astype(F32)
    fresh = jnp.where(count > 0, (1.0 - gate) * cand + gate * old, old).astype(BF)
    for part in range(out_ref.parts):
        at = slice(part * step, (part + 1) * step)
        moved = dot(put[at, :], fresh)
        out_ref[at, :] = (base_ref[at, :].astype(F32) + moved).astype(BF)
        out_ref.send(part)


def per_device(
    memory,
    ev_time,
    nbr_time,
    edge_feat,
    self_slot,
    nbr_slot,
    serve_self,
    serve_rows,
    freq,
    phase,
    w_query,
    w_key,
    w_value,
    w_out,
    w_self,
    w_msg_self,
    w_msg_other,
    w_msg_time,
    w_msg_edge,
    w_in,
    w_hid,
):
    owned, width = memory.shape
    half = w_out.shape[0]
    peers, cap = serve_rows.shape[1:]
    cap_self = serve_self.shape[2]
    events, _, neigh = nbr_slot.shape
    ends = 2 * events
    tdim = freq.shape[0]
    slots_n, slots_s = peers * cap, peers * cap_self
    packed = cap % 16 == 0 and cap_self % 16 == 0
    shape = jax.ShapeDtypeStruct

    core = lax.axis_index("mp")

    def call(kernel, out_shape, args, flops=0, scratch=(), limit=62, direct=(), views={}, parts=(), small=False, late=()):
        single = not isinstance(out_shape, (list, tuple))
        outs = [out_shape] if single else list(out_shape)
        parts = [*parts, *[1] * (len(outs) - len(parts))]
        size = sum(a.size * a.dtype.itemsize for a in (*args, *outs))
        whole, rooms = [], []
        for n, arg in enumerate(args):
            if n in direct:
                whole.append(None)
                continue
            view, room = views.get(n, (lambda ref: ref, arg.shape))
            whole.append(view)
            rooms.append(pltpu.VMEM(room, arg.dtype))
        rooms += [pltpu.VMEM(o.shape, o.dtype) for o in outs]
        return pl.pallas_call(
            functools.partial(staged, kernel, whole, parts, late),
            out_shape=out_shape,
            in_specs=[HBM if view else VMEM for view in whole],
            out_specs=HBM if single else [HBM] * len(outs),
            scratch_shapes=[
                *rooms,
                *scratch,
                pltpu.SemaphoreType.DMA((len(args),)),
                pltpu.SemaphoreType.DMA((len(outs), max(parts))),
            ],
            compiler_params=pltpu.CompilerParams(vmem_limit_bytes=int(limit * 1024 * 1024)),
            cost_estimate=pl.CostEstimate(
                flops=int(flops), bytes_accessed=1 if small else int(size), transcendentals=0
            ),
        )(*args)

    def plain(kernel, out_shape, args, flops, limit):
        size = sum(a.size * a.dtype.itemsize for a in (*args, out_shape))
        return pl.pallas_call(
            kernel,
            out_shape=out_shape,
            in_specs=[VMEM] * len(args),
            out_specs=VMEM,
            compiler_params=pltpu.CompilerParams(vmem_limit_bytes=int(limit * 1024 * 1024)),
            cost_estimate=pl.CostEstimate(
                flops=int(flops), bytes_accessed=int(size), transcendentals=0
            ),
        )(*args)

    def columns(rows):
        return (lambda ref: ref.at[:, half_of(lax.axis_index("mp"), half)], (rows, half))

    def stripe(part, size):
        return (
            lambda ref: ref.at[pl.ds(part * size, size), half_of(lax.axis_index("mp"), half)],
            (size, half),
        )

    def swap(x):
        return lax.ppermute(x, "mp", [(0, 1), (1, 0)])

    def exchange(x):
        return lax.all_to_all(x, "nodes", split_axis=0, concat_axis=0, tiled=True)

    flops_serve = 2 * (slots_n + slots_s) * owned * half
    if packed:
        served_shape = shape((peers, cap + cap_self, half), BF)
    else:
        served_shape = [shape((slots_n, half), BF), shape((slots_s, half), BF)]
    quarter = owned
    served = call(
        functools.partial(serve_kernel, packed),
        served_shape,
        (serve_rows, serve_self, memory),
        flops_serve,
        [pltpu.VMEM((1024, owned), BF)],
        views={2 + n: stripe(n, quarter) for n in range(1)},
        parts=[slots_s // 256] if packed and cap == cap_self else (),
    )
    if packed:
        old = served
        old_view = (lambda ref: ref.at[:, pl.ds(cap, cap_self), :], (peers, cap_self, half))
    else:
        served_n, old = served
        old_view = (lambda ref: ref, old.shape)
        served = jnp.concatenate(
            [served_n.reshape(peers, cap, half), old.reshape(peers, cap_self, half)], axis=1
        )
    fetched = exchange(served)

    away = lax.dynamic_slice_in_dim(
        jnp.concatenate([w_msg_self, w_msg_other, w_msg_time, w_msg_edge], axis=0),
        (1 - core) * half,
        half,
        1,
    )
    w_swap = swap(away)
    edge_t = edge_feat.T
    edge_swap = swap(edge_t)
    nslot = nbr_slot.transpose(1, 2, 0)
    slot_t = self_slot.T
    gh, te, wq_t, wkv_t, base, kvte = call(
        prepare_kernel,
        [
            shape((3, slots_s, half), F32),
            shape((1, tdim, ends), BF),
            shape((half, width + tdim), BF),
            shape((2 * half, width + tdim), BF),
            shape((owned, half), BF),
            shape((neigh + 3, 2 * half, ends), BF),
        ],
        (
            serve_self,
            ev_time[None],
            nbr_time.transpose(1, 2, 0),
            freq[None],
            phase[None],
            memory,
            w_hid.transpose(1, 0, 2),
            w_query,
            w_key,
            w_value,
            w_in.transpose(1, 0, 2),
        ),
        2 * slots_s * (owned * width + width * 3 * half),
        parts=[1, 1, 1, 1, 8, neigh + 3],
    )
    tpart = w_msg_time.shape[0]
    pack = call(
        functools.partial(slot_kernel, peers),
        shape((slots_s, pack_places(slots_s, half)[-1]), BF),
        (
            slot_t,
            te,
            edge_t,
            edge_swap,
            w_msg_time,
            w_msg_edge,
            w_msg_self,
            w_msg_other,
            w_swap,
        ),
        4 * slots_s * events * (slots_s + half),
        limit=50,
        views={
            4: columns(tpart),
            5: columns(w_msg_edge.shape[0]),
            6: columns(half),
            7: columns(half),
        },
    )
    fetched, kvte, pack, gh, base = lax.optimization_barrier((fetched, kvte, pack, gh, base))
    fetched_x = swap(fetched)
    if packed:
        both = (fetched, fetched_x)
        mine = (fetched, fetched_x)
        back_shape = shape((peers, 8, cap_self // 8 * half + 128), BF)
    else:
        nbr = [f[:, :cap].reshape(slots_n, half) for f in (fetched, fetched_x)]
        mine = [f[:, cap:].reshape(slots_s, half) for f in (fetched, fetched_x)]
        both = (nbr[0], mine[0], nbr[1], mine[1])
        back_shape = shape((slots_s, half), BF)
    total = plain(
        functools.partial(own_message_kernel, packed, cap, cap_self),
        shape((slots_s, half), F32),
        (mine[0], pack),
        slots_s * half * (2 * width + slots_s),
        50,
    )
    message = plain(
        functools.partial(message_kernel, packed, peers, cap, cap_self),
        back_shape,
        (mine[1], pack, total),
        slots_s * half * (2 * width + slots_s),
        50,
    )
    message, slot_t2 = lax.optimization_barrier((message, slot_t))
    part = call(
        functools.partial(attention_kernel, packed, cap, cap_self),
        shape((ends, width), BF),
        (*both, wkv_t, nslot, wq_t, slot_t2, phase[None], w_out, w_self, *[kvte] * 4),
        2 * ends * neigh * (slots_n + tdim) * width,
        [pltpu.VMEM((2 * half, slots_n), BF), pltpu.VMEM((neigh, half, ends), BF)],
        direct=range(len(both)),
        late=[len(both) + n for n in range(5, 11)],
        views={
            len(both) + 7 + n: (
                lambda ref, n=n: ref.at[pl.ds(n * (neigh // 4), neigh // 4)],
                (neigh // 4, 2 * half, ends),
            )
            for n in range(4)
        },
        limit=53,
    )
    part, gh, base = lax.optimization_barrier((part, gh, base))
    ready = plain(touch_kernel, shape((8, 128), F32), (gh,), 0, 49)
    embedding = call(
        sum_kernel, shape((events, 2, width), BF), (part, swap(part), ready), direct=(0, 1, 2), small=True, limit=49
    )
    if not packed:
        message = jnp.concatenate(
            [
                message.reshape(peers, cap_self, half),
                jnp.pad(pack[:peers, -128:], ((0, 0), (0, half - 128)))[:, None],
            ],
            axis=1,
        )
    back = exchange(message)
    back, embedding = lax.optimization_barrier((back, embedding))
    back_x = swap(back)
    counts = back
    if not packed:
        back_x = back_x[:, :cap_self].reshape(slots_s, half)
        counts = back[:, cap_self, :128]
        back = back[:, :cap_self].reshape(slots_s, half)
    memory_out = call(
        functools.partial(update_kernel, packed, cap_self),
        shape((owned, half), BF),
        (back, back_x, counts, serve_self, kvte, gh, old, base),
        2 * slots_s * (slots_s * width + width * 3 * half + owned * half),
        [pltpu.VMEM((owned, slots_s), BF)],
        direct=(0,1,2,5,6,7),
        views={4: (lambda ref: ref.at[pl.ds(neigh, 3)], (3, width, half))},
        parts=[8],
        limit=49,
    )
    return (embedding, memory_out)


def solution(mesh):
    return jax.shard_map(
        per_device,
        mesh=mesh,
        in_specs=(
            P("nodes", None),
            P("nodes"),
            P("nodes", None, None),
            P("nodes", "mp"),
            P("nodes", None),
            P("nodes", None, None),
            P("nodes", None, None),
            P("nodes", None, None),
            P(),
            P(),
            P(None, "mp"),
            P(None, "mp"),
            P(None, "mp"),
            P("mp", None),
            P("mp", None),
            P("mp", None),
            P("mp", None),
            P("mp", None),
            P("mp", None),
            P(None, None, "mp"),
            P(None, None, "mp"),
        ),
        out_specs=(P("nodes", None, None), P("nodes", "mp")),
        check_vma=False,
    )
```

```python
import functools

import jax
import jax.numpy as jnp
from jax import lax
from jax.experimental import pallas as pl
from jax.experimental.pallas import tpu as pltpu
from jax.sharding import PartitionSpec as P

HEADS = 8
BF = jnp.bfloat16
F32 = jnp.float32
I32 = jnp.int32
VMEM = pl.BlockSpec(memory_space=pltpu.VMEM)
HBM = pl.BlockSpec(memory_space=pltpu.HBM)
TURN = 6.283185307179586
COS = (
    6.52861337,
    -25.9675685,
    60.1676231,
    -85.4501386,
    64.9391174,
    -19.7392045,
    0.999999989,
)


def dot(a, b):
    return jnp.dot(a, b, preferred_element_type=F32)


def dot_nt(a, b):
    return lax.dot_general(a, b, (((1,), (1,)), ((), ())), preferred_element_type=F32)


def iota(shape, dim):
    return lax.broadcasted_iota(I32, shape, dim)


class Operand:
    def __init__(self, copy, ref):
        self.copy, self.ref, self.shape = copy, ref, ref.shape
        self.started = False

    def start(self):
        if not self.started:
            self.copy.start()
            self.started = True

    def wait(self):
        if self.copy is not None:
            self.start()
            self.copy.wait()
            self.copy = None

    def __getitem__(self, at):
        self.wait()
        return self.ref[at]


class Result:
    def __init__(self, room, ref, sems, parts):
        self.room, self.ref, self.sems, self.parts = room, ref, sems, parts
        self.shape, self.sent = room.shape, []

    def __setitem__(self, at, value):
        self.room[at] = value

    def __getitem__(self, at):
        return self.room[at]

    def send(self, part):
        size = self.shape[0] // self.parts
        at = pl.ds(part * size, size)
        copy = pltpu.make_async_copy(self.room.at[at], self.ref.at[at], self.sems.at[part])
        copy.start()
        self.sent.append((part, copy))

    def finish(self):
        done = [part for part, _ in self.sent]
        for part in range(self.parts):
            if part not in done:
                self.send(part)
        for _, copy in self.sent:
            copy.wait()


def staged(kernel, views, parts, late, *refs):
    count, outs = len(views), len(parts)
    ins, results, rest = refs[:count], refs[count : count + outs], list(refs[count + outs :])
    in_sems, out_sems = rest[-2:]
    rest = rest[:-2]
    operands = []
    for n, (ref, view) in enumerate(zip(ins, views)):
        if view is None:
            operands.append(ref)
        else:
            room = rest.pop(0)
            operands.append(Operand(pltpu.make_async_copy(view(ref), room, in_sems.at[n]), room))
    for n, operand in enumerate(operands):
        if isinstance(operand, Operand) and n not in late:
            operand.start()
    held = [
        Result(rest.pop(0), ref, out_sems.at[n], part)
        for n, (ref, part) in enumerate(zip(results, parts))
    ]
    kernel(*operands, *held, *rest)
    for operand in operands:
        if isinstance(operand, Operand):
            operand.wait()
    for result in held:
        result.finish()


def one_hot(mask):
    return jnp.where(mask, 1.0, 0.0).astype(BF)


def split(serve):
    high = lax.shift_right_logical(serve, 8)
    low = jnp.bitwise_and(serve, 255)
    return high.astype(F32).astype(BF), low.astype(F32).astype(BF)


def column(serve, start, count):
    peers, cap = serve.shape
    high, low = split(serve)
    pick = one_hot((iota((count, peers), 0) + start) // cap == iota((count, peers), 1))
    every = 256.0 * dot(pick, high) + dot(pick, low)
    mine = (iota((count, cap), 0) + start) % cap == iota((count, cap), 1)
    return jnp.sum(jnp.where(mine, every, 0.0), axis=1, keepdims=True)


def row(serve):
    peers, cap = serve.shape
    slots = peers * cap
    high, low = split(serve)
    pick = one_hot(iota((cap, slots), 1) % cap == iota((cap, slots), 0))
    every = 256.0 * dot(high, pick) + dot(low, pick)
    mine = iota((peers, slots), 1) // cap == iota((peers, slots), 0)
    return jnp.sum(jnp.where(mine, every, 0.0), axis=0, keepdims=True)


def hot_rows(line, start, count):
    width = line.shape[1]
    near = (line - start).astype(I32)
    near = jnp.where((near >= 0) & (near < count), near, -1)
    near = jnp.broadcast_to(near, (16, width)).astype(jnp.int16)
    near = jnp.concatenate([near] * (count // 16), axis=0)
    at = lax.broadcasted_iota(jnp.int16, (count, width), 0)
    return jnp.where(at == near, jnp.ones((), BF), jnp.zeros((), BF))


def rows_at(col, count):
    near = jnp.broadcast_to(col, (col.shape[0], 128)).astype(I32).astype(jnp.int16)
    near = jnp.concatenate([near] * (count // 128), axis=1)
    at = lax.broadcasted_iota(jnp.int16, near.shape, 1)
    return jnp.where(at == near, jnp.ones((), BF), jnp.zeros((), BF))


def half_of(core, half):
    return pl.ds(pl.multiple_of(core * half, half), half)


def serve_kernel(packed, rows_ref, self_ref, *refs):
    mems, outs, hot = refs[:1], refs[1:-1], refs[-1]
    depth, half = mems[0].shape
    count = len(mems) * depth
    step = 256
    rows, own = rows_ref[0], self_ref[0]
    jobs = []
    for table, serve in enumerate((rows, own)):
        jobs += [(start, table, serve) for start in range(0, serve.size, step)]
    jobs.sort(key=lambda job: (job[0], job[1]))
    early = hot.shape[0] // step
    for n, (start, table, serve) in enumerate(jobs[:early]):
        hot[n * step : (n + 1) * step, :] = rows_at(column(serve, start, step), count)
    for n, (start, table, serve) in enumerate(jobs):
        if n < early:
            at = hot[n * step : (n + 1) * step, :]
        else:
            at = rows_at(column(serve, start, step), count)
        picked = dot(at[:, :depth], mems[0][...])
        for part in range(1, len(mems)):
            picked = picked + dot(at[:, part * depth : (part + 1) * depth], mems[part][...])
        picked = picked.astype(BF)
        if packed:
            cap = serve.shape[1]
            first = table * rows.shape[1]
            outs[0][start // cap : (start + step) // cap, first : first + cap, :] = picked.reshape(
                step // cap, cap, half
            )
            if outs[0].parts > 1 and table == 1:
                outs[0].send(start // step)
        else:
            outs[table][start : start + step, :] = picked


def encode_turns(x):
    turns = x * (1.0 / TURN)
    u = turns - jnp.round(turns)
    square = u * u
    total = jnp.full_like(square, COS[0])
    for factor in COS[1:]:
        total = total * square + factor
    return total


def down(line, count):
    return jnp.broadcast_to(line, (count, line.shape[1])).T


def time_kernel(ev_ref, nbr_ref, freq_ref, phase_ref, wq_ref, wk_ref, wv_ref, te_ref, wqt_ref, wkvt_ref):
    neigh, tdim, ends = te_ref.shape
    events = ends // 2
    freq = down(freq_ref[...], events)
    phase = down(phase_ref[...], events)
    time = ev_ref[...]
    for k in range(neigh):
        for j in range(2):
            delta = (time - nbr_ref[j, k : k + 1, :]).astype(F32)
            enc = encode_turns(delta * freq + phase)
            te_ref[k, :, j * events : (j + 1) * events] = enc.astype(BF)
    half = wq_ref.shape[1]
    wqt_ref[...] = wq_ref[...].T
    wkvt_ref[:half, :] = wk_ref[...].T
    wkvt_ref[half:, :] = wv_ref[...].T


def tall_one_hot(slot_t_ref, slots):
    events = slot_t_ref.shape[1]
    at = iota((slots, events), 0)
    return [one_hot(at == slot_t_ref[j : j + 1, :]) for j in range(2)]


def pack_places(slots, half):
    at_pre = slots + 128
    at_weight = at_pre + 2 * half
    at_sent = at_weight + 2 * half
    return slots, at_pre, at_weight, at_sent, at_sent + 128


def slot_kernel(
    peers,
    slot_t_ref,
    te_ref,
    edge_ref,
    edge_x_ref,
    wt_ref,
    we_ref,
    ws_ref,
    wo_ref,
    wx_ref,
    pack_ref,
):
    core = lax.axis_index("mp")
    slots = pack_ref.shape[0]
    part, half = wt_ref.shape
    tall = tall_one_hot(slot_t_ref, slots)
    events = tall[0].shape[1]
    both = tall[0] + tall[1]
    at_count, at_pre, at_weight, at_sent = pack_places(slots, half)[:4]
    pack_ref[:, :at_count] = (dot_nt(tall[0], tall[1]) + dot_nt(tall[1], tall[0])).astype(BF)
    count = dot_nt(both, jnp.ones((128, events), BF))
    pack_ref[:, at_count:at_pre] = count.astype(BF)
    cap = slots // peers
    place = iota((slots, 128), 0) % cap == iota((slots, 128), 1)
    owner = one_hot(iota((peers, slots), 1) // cap == iota((peers, slots), 0))
    pack_ref[:peers, at_sent:] = dot(owner, jnp.where(place, count, 0.0).astype(BF)).astype(BF)
    pack_ref[peers:, at_sent:] = jnp.zeros((slots - peers, 128), BF)
    pack_ref[:half, at_weight : at_weight + half] = wo_ref[...]
    pack_ref[:half, at_weight + half : at_sent] = ws_ref[...]
    pack_ref[half : 2 * half, at_weight : at_weight + half] = wx_ref[half : 2 * half, :]
    pack_ref[half : 2 * half, at_weight + half : at_sent] = wx_ref[:half, :]
    mine, theirs = wt_ref[...], wx_ref[2 * half : 2 * half + part, :]
    first = core == 0
    weight = jnp.concatenate(
        [
            jnp.where(first, mine, theirs),
            jnp.where(first, theirs, mine),
            we_ref[...],
            wx_ref[2 * half + part :, :],
        ],
        axis=0,
    )
    edge = jnp.concatenate([edge_ref[...], edge_x_ref[...]], axis=0)
    value = jnp.concatenate(
        [dot_nt(jnp.concatenate(tall, axis=1), te_ref[0]), dot_nt(both, edge)], axis=1
    )
    high = value.astype(BF)
    low = (value - high.astype(F32)).astype(BF)
    pre = dot(high, weight) + dot(low, weight)
    high = pre.astype(BF)
    pack_ref[:, at_pre : at_pre + half] = high
    pack_ref[:, at_pre + half : at_weight] = (pre - high.astype(F32)).astype(BF)


def prepare_kernel(
    self_ref,
    ev_ref,
    nbr_ref,
    freq_ref,
    phase_ref,
    mem_ref,
    whid_ref,
    wq_ref,
    wk_ref,
    wv_ref,
    gh_ref,
    te_ref,
    wqt_ref,
    wkvt_ref,
    base_ref,
):
    time_kernel(ev_ref, nbr_ref, freq_ref, phase_ref, wq_ref, wk_ref, wv_ref, te_ref, wqt_ref, wkvt_ref)
    te_ref.send(0)
    wqt_ref.send(0)
    wkvt_ref.send(0)
    count, width = mem_ref.shape
    serve = self_ref[0]
    slots = serve.size
    col = column(serve, 0, slots)
    for start in range(0, slots, 256):
        at = slice(start, start + 256)
        picked = dot(rows_at(col[at], count), mem_ref[...]).astype(BF)
        for g in range(3):
            gh_ref[g, at, :] = dot(picked, whid_ref[g])
    gh_ref.send(0)
    line = row(serve)
    cols = half_of(lax.axis_index("mp"), width // 2)
    step = count // base_ref.parts
    for part in range(base_ref.parts):
        at = slice(part * step, (part + 1) * step)
        hit = hot_rows(line, part * step, step)
        served = dot(hit, jnp.ones((slots, 128), BF))
        free = jnp.concatenate([jnp.where(served > 0, 0.0, 1.0)] * (width // 256), axis=1)
        base_ref[at, :] = (mem_ref[at, cols].astype(F32) * free).astype(BF)
        base_ref.send(part)


def part_of(ref, packed, start, size):
    if packed:
        return ref[:, start : start + size, :].reshape(-1, ref.shape[2])
    return ref[...]


def message_part(own, pack_ref, first, half):
    slots = pack_ref.shape[0]
    at_count, at_pre, at_weight, at_sent, _ = pack_places(slots, half)
    both = dot(own, pack_ref[first : first + half, at_weight:at_sent])
    count = pack_ref[:, at_count:at_pre].astype(F32)
    count = jnp.concatenate([count] * (half // 128), axis=1)
    return dot(pack_ref[:, :at_count], both[:, :half].astype(BF)) + count * both[:, half:]


def own_message_kernel(packed, cap, cap_self, own_ref, pack_ref, total_ref):
    half = own_ref.shape[-1]
    _, at_pre, at_weight, _, _ = pack_places(pack_ref.shape[0], half)
    pre = pack_ref[:, at_pre : at_pre + half].astype(F32)
    pre = pre + pack_ref[:, at_pre + half : at_weight].astype(F32)
    own = part_of(own_ref, packed, cap, cap_self)
    total_ref[...] = message_part(own, pack_ref, 0, half) + pre


def message_kernel(packed, peers, cap, cap_self, oth_ref, pack_ref, total_ref, out_ref):
    half = oth_ref.shape[-1]
    at_sent = pack_places(pack_ref.shape[0], half)[3]
    oth = part_of(oth_ref, packed, cap, cap_self)
    out = (total_ref[...] + message_part(oth, pack_ref, half, half)).astype(BF)
    if not packed:
        out_ref[...] = out
        return
    tiles = half // 128
    for tile in range(tiles):
        out_ref[:, tile * cap_self : (tile + 1) * cap_self, :] = out[
            :, tile * 128 : (tile + 1) * 128
        ].reshape(peers, cap_self, 128)
    sent = pack_ref[:peers, at_sent:].astype(F32)
    out_ref[:, tiles * cap_self :, :] = jnp.broadcast_to(sent[:, None, :], (peers, 16, 128)).astype(
        BF
    )


def attention_kernel(
    packed,
    cap,
    cap_self,
    *refs,
):
    own_refs, oth_refs, refs = (refs[:1], refs[1:2], refs[2:]) if packed else (
        refs[:2], refs[2:4], refs[4:]
    )
    wkvt_ref, nslot_ref, te_ref, wqt_ref, slot_t_ref, phase_ref, wout_ref, wself_ref = refs[:8]
    emb_ref, kv_w, value_ref = refs[8:]
    nown_ref, sown_ref = own_refs[0], own_refs[-1]
    noth_ref, soth_ref = oth_refs[0], oth_refs[-1]
    core = lax.axis_index("mp")
    half = wout_ref.shape[0]
    width = 2 * half
    size = width // HEADS
    heads = HEADS // 2
    mine, theirs = half_of(core, half), half_of(1 - core, half)
    fown = part_of(nown_ref, packed, 0, cap)
    foth = part_of(noth_ref, packed, 0, cap)
    for ref in (te_ref, wout_ref, wself_ref):
        ref.start()
    slots = fown.shape[0]
    kv_w[:, :slots] = (dot_nt(wkvt_ref[:, mine], fown) + dot_nt(wkvt_ref[:, theirs], foth)).astype(BF)
    kv_w[:, slots:] = wkvt_ref[:, width:]
    xown = part_of(sown_ref, packed, cap, cap_self)
    xoth = part_of(soth_ref, packed, cap, cap_self)
    slots_s = xown.shape[0]
    te_self = encode_turns(phase_ref[...]).astype(BF)
    te_self = jnp.broadcast_to(te_self, (128, te_self.shape[1]))
    query = dot_nt(wqt_ref[:, mine], xown) + dot_nt(wqt_ref[:, theirs], xoth)
    query_te = dot_nt(wqt_ref[:, width:], te_self)
    query = (query + jnp.concatenate([query_te] * (slots_s // 128), axis=1)).astype(BF)
    find = jnp.concatenate(tall_one_hot(slot_t_ref, slots_s), axis=1)
    q = dot(query, find) * (1.0 / size**0.5)
    neigh, _, ends = te_ref.shape
    at = lax.broadcasted_iota(jnp.int16, (slots, ends), 0)
    one, zero = jnp.ones((), BF), jnp.zeros((), BF)
    weights = []
    for k in range(neigh):
        line = jnp.concatenate([nslot_ref[j, k : k + 1, :] for j in range(2)], axis=1)
        line = jnp.broadcast_to(line, (16, ends)).astype(jnp.int16)
        line = jnp.concatenate([line] * (slots // 16), axis=0)
        hot = jnp.where(at == line, one, zero)
        right = jnp.concatenate([hot, te_ref[k]], axis=0)
        kv = dot(kv_w[...], right)
        value_ref[k] = kv[half:].astype(BF)
        score = q * kv[:half]
        score = [
            jnp.sum(score[h * size : (h + 1) * size], axis=0, keepdims=True) for h in range(heads)
        ]
        weights.append(jnp.exp(jnp.concatenate(score, axis=0)))
    total = weights[0]
    for k in range(1, neigh):
        total = total + weights[k]
    weights = [(w / total).astype(BF).astype(F32) for w in weights]
    att = []
    for h in range(heads):
        part = jnp.zeros((size, ends), F32)
        for k in range(neigh):
            value = value_ref[k, h * size : (h + 1) * size, :].astype(F32)
            part = part + weights[k][h : h + 1] * value
        att.append(part)
    att = jnp.concatenate(att, axis=0).T.astype(BF)
    events = ends // 2
    at = iota((events, slots_s), 1)
    find = [
        one_hot(at == down(slot_t_ref[j : j + 1, :].astype(F32), slots_s).astype(I32))
        for j in range(2)
    ]
    self_own = dot(jnp.concatenate(find, axis=0), xown).astype(BF)
    emb_ref[...] = (dot(att, wout_ref[...]) + dot(self_own, wself_ref[...])).astype(BF)


def sum_kernel(own_ref, oth_ref, out_ref):
    total = own_ref[...].astype(F32) + oth_ref[...].astype(F32)
    events = out_ref.shape[0]
    out_ref[...] = jnp.stack([total[:events], total[events:]], axis=1).astype(BF)


def update_kernel(
    packed,
    cap_self,
    own_ref,
    oth_ref,
    count_ref,
    serve_ref,
    win_ref,
    gh_ref,
    old_ref,
    base_ref,
    out_ref,
    put,
):
    core = lax.axis_index("mp")
    rows, half = base_ref.shape
    serve = serve_ref[0]
    slots = serve.size
    tiles = half // 128

    def messages(ref):
        if not packed:
            return ref[...]
        return jnp.concatenate(
            [
                ref[:, tile * cap_self : (tile + 1) * cap_self, :].reshape(slots, 128)
                for tile in range(tiles)
            ],
            axis=1,
        )

    line = row(serve)
    match = column(serve, 0, slots) == line
    same = one_hot(match)
    earlier = match & (iota((slots, slots), 0) < iota((slots, slots), 1))
    again = jnp.sum(jnp.where(earlier, 1.0, 0.0), axis=0, keepdims=True)
    line = jnp.where(again > 0, -1.0, line)
    step = rows // out_ref.parts
    for part in range(out_ref.parts):
        put[part * step : (part + 1) * step, :] = hot_rows(line, part * step, step)
    peers = slots // cap_self
    counts = count_ref[:, tiles * cap_self :, :][:, 0, :] if packed else count_ref[...]
    spread = dot(one_hot(iota((slots, peers), 0) // cap_self == iota((slots, peers), 1)), counts)
    lane = iota((slots, 128), 1)
    spread = jnp.where(iota((slots, 128), 0) % cap_self == lane, spread, 0.0).astype(BF)
    count = jnp.sum(dot(same, spread), axis=1, keepdims=True)
    inverse = 1.0 / jnp.maximum(count, 1.0)
    own = (dot(same, messages(own_ref)) * inverse).astype(BF)
    oth = (dot(same, messages(oth_ref)) * inverse).astype(BF)
    mine, theirs = half_of(core, half), half_of(1 - core, half)
    gi = [dot(own, win_ref[g, mine, :]) + dot(oth, win_ref[g, theirs, :]) for g in range(3)]
    reset = jax.nn.sigmoid(gi[0] + gh_ref[0])
    gate = jax.nn.sigmoid(gi[1] + gh_ref[1])
    cand = jnp.tanh(gi[2] + reset * gh_ref[2])
    old = old_ref[...].reshape(slots, half).astype(F32)
    fresh = jnp.where(count > 0, (1.0 - gate) * cand + gate * old, old).astype(BF)
    for part in range(out_ref.parts):
        at = slice(part * step, (part + 1) * step)
        moved = dot(put[at, :], fresh)
        out_ref[at, :] = (base_ref[at, :].astype(F32) + moved).astype(BF)
        out_ref.send(part)


def per_device(
    memory,
    ev_time,
    nbr_time,
    edge_feat,
    self_slot,
    nbr_slot,
    serve_self,
    serve_rows,
    freq,
    phase,
    w_query,
    w_key,
    w_value,
    w_out,
    w_self,
    w_msg_self,
    w_msg_other,
    w_msg_time,
    w_msg_edge,
    w_in,
    w_hid,
):
    owned, width = memory.shape
    half = w_out.shape[0]
    peers, cap = serve_rows.shape[1:]
    cap_self = serve_self.shape[2]
    events, _, neigh = nbr_slot.shape
    ends = 2 * events
    tdim = freq.shape[0]
    slots_n, slots_s = peers * cap, peers * cap_self
    packed = cap % 16 == 0 and cap_self % 16 == 0
    shape = jax.ShapeDtypeStruct

    core = lax.axis_index("mp")

    def call(kernel, out_shape, args, flops=0, scratch=(), limit=62, direct=(), views={}, parts=(), small=False, late=()):
        single = not isinstance(out_shape, (list, tuple))
        outs = [out_shape] if single else list(out_shape)
        parts = [*parts, *[1] * (len(outs) - len(parts))]
        size = sum(a.size * a.dtype.itemsize for a in (*args, *outs))
        whole, rooms = [], []
        for n, arg in enumerate(args):
            if n in direct:
                whole.append(None)
                continue
            view, room = views.get(n, (lambda ref: ref, arg.shape))
            whole.append(view)
            rooms.append(pltpu.VMEM(room, arg.dtype))
        rooms += [pltpu.VMEM(o.shape, o.dtype) for o in outs]
        return pl.pallas_call(
            functools.partial(staged, kernel, whole, parts, late),
            out_shape=out_shape,
            in_specs=[HBM if view else VMEM for view in whole],
            out_specs=HBM if single else [HBM] * len(outs),
            scratch_shapes=[
                *rooms,
                *scratch,
                pltpu.SemaphoreType.DMA((len(args),)),
                pltpu.SemaphoreType.DMA((len(outs), max(parts))),
            ],
            compiler_params=pltpu.CompilerParams(vmem_limit_bytes=limit * 1024 * 1024),
            cost_estimate=pl.CostEstimate(
                flops=int(flops), bytes_accessed=1 if small else int(size), transcendentals=0
            ),
        )(*args)

    def plain(kernel, out_shape, args, flops, limit):
        size = sum(a.size * a.dtype.itemsize for a in (*args, out_shape))
        return pl.pallas_call(
            kernel,
            out_shape=out_shape,
            in_specs=[VMEM] * len(args),
            out_specs=VMEM,
            compiler_params=pltpu.CompilerParams(vmem_limit_bytes=limit * 1024 * 1024),
            cost_estimate=pl.CostEstimate(
                flops=int(flops), bytes_accessed=int(size), transcendentals=0
            ),
        )(*args)

    def columns(rows):
        return (lambda ref: ref.at[:, half_of(lax.axis_index("mp"), half)], (rows, half))

    def stripe(part, size):
        return (
            lambda ref: ref.at[pl.ds(part * size, size), half_of(lax.axis_index("mp"), half)],
            (size, half),
        )

    def swap(x):
        return lax.ppermute(x, "mp", [(0, 1), (1, 0)])

    def exchange(x):
        return lax.all_to_all(x, "nodes", split_axis=0, concat_axis=0, tiled=True)

    flops_serve = 2 * (slots_n + slots_s) * owned * half
    if packed:
        served_shape = shape((peers, cap + cap_self, half), BF)
    else:
        served_shape = [shape((slots_n, half), BF), shape((slots_s, half), BF)]
    quarter = owned
    served = call(
        functools.partial(serve_kernel, packed),
        served_shape,
        (serve_rows, serve_self, memory),
        flops_serve,
        [pltpu.VMEM((1024, owned), BF)],
        views={2 + n: stripe(n, quarter) for n in range(1)},
        parts=[slots_s // 256] if packed and cap == cap_self else (),
    )
    if packed:
        old = served
        old_view = (lambda ref: ref.at[:, pl.ds(cap, cap_self), :], (peers, cap_self, half))
    else:
        served_n, old = served
        old_view = (lambda ref: ref, old.shape)
        served = jnp.concatenate(
            [served_n.reshape(peers, cap, half), old.reshape(peers, cap_self, half)], axis=1
        )
    fetched = exchange(served)

    away = lax.dynamic_slice_in_dim(
        jnp.concatenate([w_msg_self, w_msg_other, w_msg_time, w_msg_edge], axis=0),
        (1 - core) * half,
        half,
        1,
    )
    w_swap = swap(away)
    edge_t = edge_feat.T
    edge_swap = swap(edge_t)
    nslot = nbr_slot.transpose(1, 2, 0)
    slot_t = self_slot.T
    gh, te, wq_t, wkv_t, base = call(
        prepare_kernel,
        [
            shape((3, slots_s, half), F32),
            shape((neigh, tdim, ends), BF),
            shape((half, width + tdim), BF),
            shape((2 * half, width + tdim), BF),
            shape((owned, half), BF),
        ],
        (
            serve_self,
            ev_time[None],
            nbr_time.transpose(1, 2, 0),
            freq[None],
            phase[None],
            memory,
            w_hid.transpose(1, 0, 2),
            w_query,
            w_key,
            w_value,
        ),
        2 * slots_s * (owned * width + width * 3 * half),
        parts=[1, 1, 1, 1, 8],
    )
    tpart = w_msg_time.shape[0]
    pack = call(
        functools.partial(slot_kernel, peers),
        shape((slots_s, pack_places(slots_s, half)[-1]), BF),
        (
            slot_t,
            te,
            edge_t,
            edge_swap,
            w_msg_time,
            w_msg_edge,
            w_msg_self,
            w_msg_other,
            w_swap,
        ),
        4 * slots_s * events * (slots_s + half),
        limit=50,
        views={
            1: (lambda ref: ref.at[pl.ds(0, 1)], (1, tdim, ends)),
            4: columns(tpart),
            5: columns(w_msg_edge.shape[0]),
            6: columns(half),
            7: columns(half),
        },
    )
    fetched, te, pack, gh, base = lax.optimization_barrier((fetched, te, pack, gh, base))
    fetched_x = swap(fetched)
    if packed:
        both = (fetched, fetched_x)
        mine = (fetched, fetched_x)
        back_shape = shape((peers, (half // 128) * cap_self + 16, 128), BF)
    else:
        nbr = [f[:, :cap].reshape(slots_n, half) for f in (fetched, fetched_x)]
        mine = [f[:, cap:].reshape(slots_s, half) for f in (fetched, fetched_x)]
        both = (nbr[0], mine[0], nbr[1], mine[1])
        back_shape = shape((slots_s, half), BF)
    total = plain(
        functools.partial(own_message_kernel, packed, cap, cap_self),
        shape((slots_s, half), F32),
        (mine[0], pack),
        slots_s * half * (2 * width + slots_s),
        50,
    )
    message = plain(
        functools.partial(message_kernel, packed, peers, cap, cap_self),
        back_shape,
        (mine[1], pack, total),
        slots_s * half * (2 * width + slots_s),
        50,
    )
    message, slot_t2 = lax.optimization_barrier((message, slot_t))
    part = call(
        functools.partial(attention_kernel, packed, cap, cap_self),
        shape((ends, width), BF),
        (*both, wkv_t, nslot, te, wq_t, slot_t2, phase[None], w_out, w_self),
        2 * ends * neigh * (slots_n + tdim) * width,
        [pltpu.VMEM((2 * half, slots_n + tdim), BF), pltpu.VMEM((neigh, half, ends), BF)],
        direct=range(len(both)),
        late=[len(both) + n for n in (2, 6, 7)],
        limit=53,
    )
    embedding = call(
        sum_kernel, shape((events, 2, width), BF), (part, swap(part)), direct=(0, 1), small=True, limit=52
    )
    if not packed:
        message = jnp.concatenate(
            [
                message.reshape(peers, cap_self, half),
                jnp.pad(pack[:peers, -128:], ((0, 0), (0, half - 128)))[:, None],
            ],
            axis=1,
        )
    back = exchange(message)
    back, embedding = lax.optimization_barrier((back, embedding))
    back_x = swap(back)
    counts = back
    if not packed:
        back_x = back_x[:, :cap_self].reshape(slots_s, half)
        counts = back[:, cap_self, :128]
        back = back[:, :cap_self].reshape(slots_s, half)
    memory_out = call(
        functools.partial(update_kernel, packed, cap_self),
        shape((owned, half), BF),
        (back, back_x, counts, serve_self, w_in.transpose(1, 0, 2), gh, old, base),
        2 * slots_s * (slots_s * width + width * 3 * half + owned * half),
        [pltpu.VMEM((owned, slots_s), BF)],
        direct=(0, 1, 2),
        views={6: old_view},
        parts=[8],
        limit=53,
    )
    return (embedding, memory_out)


def solution(mesh):
    return jax.shard_map(
        per_device,
        mesh=mesh,
        in_specs=(
            P("nodes", None),
            P("nodes"),
            P("nodes", None, None),
            P("nodes", "mp"),
            P("nodes", None),
            P("nodes", None, None),
            P("nodes", None, None),
            P("nodes", None, None),
            P(),
            P(),
            P(None, "mp"),
            P(None, "mp"),
            P(None, "mp"),
            P("mp", None),
            P("mp", None),
            P("mp", None),
            P("mp", None),
            P("mp", None),
            P("mp", None),
            P(None, None, "mp"),
            P(None, None, "mp"),
        ),
        out_specs=(P("nodes", None, None), P("nodes", "mp")),
        check_vma=False,
    )
```
